32 devices in a mesh: seq: 16 (over z, y, x), chan: 2 (over core).
Axes of the slice: x: 2, y: 2, z: 4, core: 2. Of those that a mesh axis runs over, the one named last changes fastest.
Arguments:
- streams: bfloat16 [3, 512, 4096], P(None, 'chan', 'seq'), may hold values from -6 to 6
- short_filters: float32 [3, 7, 512], P(None, None, 'chan'), may hold values from -2 to 2
- long_filter: float32 [64, 4096], P(None, 'seq'), may hold values from -2 to 2
- skip_gain: float32 [512], P('chan'), may hold values from 0.3 to 1.5
- out_grad: bfloat16 [512, 4096], P('chan', 'seq'), may hold values from -6 to 6
Outputs:
- stream_grad: bfloat16 [3, 512, 4096], P(None, 'chan', 'seq')
- filter_grad: float32 [64, 4096], P(None, 'seq')
The draws below stay inside these ranges and needn't reach their ends.
All inputs are finite; a program needn't handle non-finite values.
Results may differ from the reference program's by a relative error of at most 0.0004.
Values may be sent and summed in bfloat16 or wider, within the bound.
A program may use at most 64 MiB of HBM per device.

```python
import math
import jax
import jax.numpy as jnp

TAPS = 7
FILTERS = 64
CHANNELS = 512
TOKENS = 4096


def draw_long_filter(key, part):
    first_key, second_key = jax.random.split(key, 2)
    lags = jnp.arange(TOKENS, dtype=jnp.float32)[None, :]
    reach_len = jnp.exp(jax.random.uniform(first_key, (FILTERS, 1), jnp.float32, math.log(30.0), math.log(4.0 * TOKENS)))
    amplitude = jnp.sqrt(2.0 / jnp.minimum(reach_len, TOKENS * 1.0))
    noise = jnp.clip(jax.random.normal(second_key, (FILTERS, TOKENS), jnp.float32), -5.0, 5.0)
    return noise * amplitude * jnp.exp(-lags / reach_len)


def block_scale(own_key, shape, cuts, least, largest):
    loudness = 1.0
    for position, parts in cuts:
        heights = jax.random.uniform(jax.random.fold_in(jax.random.fold_in(own_key, 6), position), (parts,), jnp.float32, least / len(cuts), largest / len(cuts))
        loudness = loudness * jnp.repeat(jnp.exp(heights), shape[position] // parts).reshape((-1,) + (1,) * (len(shape) - 1 - position))
    return loudness


def centred(key, shape, deviation, reach, pieces=(), held_as=jnp.bfloat16):
    array = jax.random.normal(key, shape, jnp.float32) * deviation
    if len(pieces) > 0:
        array = block_scale(key, shape, pieces, -0.22, 0.18) * array
    return jnp.clip(array, min=-reach, max=reach).astype(held_as)


def setup_inputs(seed: int = 0) -> dict:
    keys = jax.random.split(jax.random.key(seed), 6)
    streams = centred(keys[0], (3, CHANNELS, TOKENS), 1.0, 6.0, ((1, 2), (2, 16)))
    short_filters = centred(keys[1], (3, TAPS, CHANNELS), TAPS ** -0.5, 2.0, ((2, 2),), jnp.float32)
    long_filter = draw_long_filter(jax.random.fold_in(keys[5], 71), 0)
    skip_gain = jnp.clip(jnp.exp(math.log(1.5) - 1.60943787 * jax.random.uniform(keys[3], (CHANNELS,), jnp.float32) ** block_scale(keys[3], (CHANNELS,), ((0, 2),), -0.2, 0.2)), 0.3, 1.5)
    out_grad = centred(keys[4], (CHANNELS, TOKENS), 1.0, 6.0, ((0, 2), (1, 16)))
    return {"streams": streams, "short_filters": short_filters, "long_filter": long_filter, "skip_gain": skip_gain, "out_grad": out_grad}


def reference(streams, short_filters, long_filter, skip_gain, out_grad):
    seq_total = streams.shape[2]
    tap_count = short_filters.shape[1]
    reach_back = tap_count - 1
    inputs_f = streams.astype(jnp.float32)
    padded = jnp.pad(inputs_f, ((0, 0), (0, 0), (reach_back, 0)))
    filtered = jnp.zeros(inputs_f.shape, jnp.float32)
    for offset in range(tap_count):
        filtered = filtered + short_filters[:, offset, :, None] * padded[:, :, reach_back - offset:reach_back - offset + seq_total]
    gate_out = filtered[0]
    gate_in = filtered[1]
    values = filtered[2]
    gated_prod = gate_in * values
    members = gate_out.shape[0] // long_filter.shape[0]
    kernel = jnp.tile(long_filter, (members, 1))
    fft_size = 2 * seq_total
    gated_spec = jnp.fft.rfft(gated_prod, n=fft_size, axis=1)
    kernel_spec = jnp.fft.rfft(kernel, n=fft_size, axis=1)
    conv_out = jnp.fft.irfft(gated_spec * kernel_spec, n=fft_size, axis=1)[:, :seq_total] + skip_gain[:, None] * gated_prod
    out_float = out_grad.astype(jnp.float32)
    gate_grad = out_float * gate_out
    grad_spec = jnp.fft.rfft(gate_grad, n=fft_size, axis=1)
    gated_grad = jnp.fft.irfft(grad_spec * jnp.conj(kernel_spec), n=fft_size, axis=1)[:, :seq_total] + skip_gain[:, None] * gate_grad
    paired = jnp.fft.irfft(grad_spec * jnp.conj(gated_spec), n=fft_size, axis=1)[:, :seq_total]
    filter_grad = paired.reshape(members, -1, seq_total).sum(axis=0) / jnp.sqrt(jnp.float32(members * seq_total))
    grads_in = jnp.stack([out_float * conv_out, gated_grad * values, gated_grad * gate_in])
    padded_grad = jnp.pad(grads_in, ((0, 0), (0, 0), (0, reach_back)))
    result = jnp.zeros(grads_in.shape, jnp.float32)
    for offset in range(tap_count):
        result = result + short_filters[:, offset, :, None] * padded_grad[:, :, offset:offset + seq_total]
    return (result.astype(jnp.bfloat16), filter_grad.astype(jnp.float32))
```

```python
import functools
import math

import jax
import jax.numpy as jnp
import ml_dtypes
import numpy as np
from jax import lax
from jax.experimental import pallas as pl
from jax.experimental.pallas import tpu as pltpu
from jax.sharding import PartitionSpec as P

MESH = pl.DeviceIdType.MESH


def partner_2(value, axis, apart):
    mask = 2**apart
    pairs = [(source, source ^ mask) for source in range(lax.axis_size(axis))]
    return lax.ppermute(value, axis, pairs)


def shifted(shard, axis, by):
    length = lax.axis_size(axis)
    pairs = [(i, i + by) for i in range(length) if 0 <= i + by < length]
    return lax.ppermute(shard, axis, pairs)


def rotate(real_part, imag_part, cosine, sine_part):
    return (real_part * cosine - imag_part * sine_part, real_part * sine_part + imag_part * cosine)


def split_halves(signal):
    middle = signal.shape[-1] // 2
    return (signal[..., :middle], signal[..., middle:])


def join_halves(real_part, imag_part):
    return jnp.concatenate([real_part, imag_part], axis=-1)


def complex_product(first_op, second_op, conjugate):
    first_re, first_im = split_halves(first_op)
    second_re, second_im = split_halves(second_op)
    if conjugate:
        second_im = -second_im
    return join_halves(
        first_re * second_re - first_im * second_im, first_re * second_im + first_im * second_re
    )


def dft_table(length, direction, scaling):
    indices = jnp.arange(length, dtype=jnp.int32)
    phases = (indices[:, None] * indices[None, :] % length).astype(jnp.float32) * (
        direction * 2.0 * math.pi / length
    )
    cosine = jnp.cos(phases) * scaling
    sine_part = jnp.sin(phases) * scaling
    upper_rows = jnp.concatenate([cosine, sine_part], axis=1)
    lower_rows = jnp.concatenate([-sine_part, cosine], axis=1)
    return jnp.concatenate([upper_rows, lower_rows], axis=0)


def section_count():
    return lax.axis_size("seq").bit_length() - 1


def bit_reverse(position, sections):
    result = jnp.zeros((), jnp.int32)
    for bit_level in range(sections):
        result = result + position // (1 << bit_level) % 2 * (1 << sections - 1 - bit_level)
    return result


def held_index():
    return bit_reverse(lax.axis_index("seq"), section_count())


def inner_twiddle(signal, held, direction):
    length = signal.shape[-1] // 2
    seq_total = length * lax.axis_size("seq")
    indices = jnp.arange(length, dtype=jnp.int32)
    phases = (indices * held % seq_total).astype(jnp.float32) * (
        direction * 2.0 * math.pi / seq_total
    )
    real_part, imag_part = split_halves(signal)
    turned_re, turned_im = rotate(real_part, imag_part, jnp.cos(phases), jnp.sin(phases))
    return join_halves(turned_re, turned_im)


def forward_sections(signal):
    position = lax.axis_index("seq")
    sections = section_count()
    for bit_level in reversed(range(sections)):
        half_span = 1 << bit_level
        partner = partner_2(signal, "seq", bit_level)
        upper_side = position // half_span % 2 == 1
        phases = (position % half_span).astype(jnp.float32) * (-math.pi / half_span)
        diff_re, diff_im = split_halves(partner - signal)
        turned_re, turned_im = rotate(diff_re, diff_im, jnp.cos(phases), jnp.sin(phases))
        signal = jnp.where(upper_side, join_halves(turned_re, turned_im), signal + partner)
    return signal


def inverse_sections(signal):
    position = lax.axis_index("seq")
    sections = section_count()
    for bit_level in range(sections):
        half_span = 1 << bit_level
        partner = partner_2(signal, "seq", bit_level)
        upper_side = position // half_span % 2 == 1
        phases = (position % half_span).astype(jnp.float32) * (math.pi / half_span)
        source = jnp.where(upper_side, signal, partner)
        base_term = jnp.where(upper_side, partner, signal)
        source_re, source_im = split_halves(source)
        turned_re, turned_im = rotate(source_re, source_im, jnp.cos(phases), jnp.sin(phases))
        turned = join_halves(turned_re, turned_im)
        signal = 0.5 * jnp.where(upper_side, base_term - turned, base_term + turned)
    return signal


def forward_dft(signal, dft_matrix):
    signal = forward_sections(signal)
    signal = inner_twiddle(signal, held_index(), -1.0)
    return jnp.dot(
        signal, dft_matrix, precision=lax.Precision.HIGHEST, preferred_element_type=jnp.float32
    )


def inverse_dft(spectra, dft_matrix):
    signal = jnp.dot(
        spectra, dft_matrix, precision=lax.Precision.HIGHEST, preferred_element_type=jnp.float32
    )
    signal = inner_twiddle(signal, held_index(), 1.0)
    return inverse_sections(signal)


def local(streams, short_filters, long_filter, skip_gain, out_grad):
    tap_count = short_filters.shape[1]
    reach_back = tap_count - 1
    channels_dev = streams.shape[1]
    length = streams.shape[2]
    filters = long_filter.shape[0]
    members = channels_dev // filters
    devices = lax.axis_size("seq")
    position = lax.axis_index("seq")
    seq_total = length * devices
    preceding = shifted(streams[:, :, length - reach_back :], "seq", 1)
    extended = jnp.concatenate([preceding, streams], axis=2).astype(jnp.float32)
    filtered = jnp.zeros(streams.shape, jnp.float32)
    for offset in range(tap_count):
        filtered = (
            filtered
            + short_filters[:, offset, :, None]
            * extended[:, :, reach_back - offset : reach_back - offset + length]
        )
    gate_out = filtered[0]
    gate_in = filtered[1]
    values = filtered[2]
    gated_prod = gate_in * values
    out_float = out_grad.astype(jnp.float32)
    gate_grad = out_float * gate_out
    signals = jnp.concatenate([gated_prod, gate_grad, long_filter], axis=0)
    twist_phase = (position * length + jnp.arange(length, dtype=jnp.int32)).astype(jnp.float32) * (
        -math.pi / seq_total
    )
    twist_re = jnp.cos(twist_phase)
    twist_im = jnp.sin(twist_phase)
    even_part = join_halves(signals, jnp.zeros_like(signals))
    odd_part = join_halves(signals * twist_re, signals * twist_im)
    spectra = forward_dft(
        jnp.concatenate([even_part, odd_part], axis=0), dft_table(length, -1.0, 1.0)
    )
    row_count = signals.shape[0]
    halves = (spectra[:row_count], spectra[row_count:])
    filter_specs = (halves[0][2 * channels_dev :], halves[1][2 * channels_dev :])
    products = []
    for half_index in range(2):
        part_spec = halves[half_index]
        gated_spec = part_spec[:channels_dev]
        grad_spec = part_spec[channels_dev : 2 * channels_dev]
        wide_filter = jnp.tile(filter_specs[half_index], (members, 1))
        products.append(complex_product(gated_spec, wide_filter, False))
        products.append(complex_product(grad_spec, wide_filter, True))
        products.append(
            complex_product(grad_spec, gated_spec, True)
            .reshape(members, filters, 2 * length)
            .sum(axis=0)
        )
    time_rows = inverse_dft(jnp.concatenate(products, axis=0), dft_table(length, 1.0, 1.0 / length))
    part_rows = 2 * channels_dev + filters
    even_re, even_im = split_halves(time_rows[:part_rows])
    odd_re, odd_im = split_halves(time_rows[part_rows:])
    combined = 0.5 * (even_re + twist_re * odd_re + twist_im * odd_im)
    conv_part = combined[:channels_dev]
    corr_part = combined[channels_dev : 2 * channels_dev]
    filter_local = combined[2 * channels_dev :]
    conv_out = conv_part + skip_gain[:, None] * gated_prod
    gated_grad = corr_part + skip_gain[:, None] * gate_grad
    members_total = channels_dev * lax.axis_size("chan") // filters
    filter_grad = lax.psum(filter_local, "chan") * (1.0 / math.sqrt(members_total * seq_total))
    grads_in = jnp.stack([out_float * conv_out, gated_grad * values, gated_grad * gate_in])
    following = shifted(grads_in[:, :, :reach_back], "seq", -1)
    extended_grad = jnp.concatenate([grads_in, following], axis=2)
    result = jnp.zeros(grads_in.shape, jnp.float32)
    for offset in range(tap_count):
        result = (
            result
            + short_filters[:, offset, :, None] * extended_grad[:, :, offset : offset + length]
        )
    return (result.astype(jnp.bfloat16), filter_grad)


BF16 = jnp.bfloat16
F32 = jnp.float32
LANES = 128


def split16(value):
    high = value.astype(BF16)
    return high, (value - high.astype(F32)).astype(BF16)


def host_split(table):
    high = table.astype(np.float32).astype(ml_dtypes.bfloat16)
    low = (table - high.astype(np.float64)).astype(np.float32).astype(ml_dtypes.bfloat16)
    return high, low


def one_hot_rows(sources):
    table = np.zeros((len(sources), len(sources)), np.float32)
    table[np.arange(len(sources)), sources] = 1.0
    return table.astype(ml_dtypes.bfloat16)


def tables(channels, filters, devices, tokens):
    members = channels // filters
    own_filters = filters // devices
    rows = np.arange(channels)
    order = one_hot_rows(filters * (rows % members) + rows // members)
    rows = np.arange(4 * filters)
    owner, kind, own = rows // (4 * own_filters), rows // own_filters % 4, rows % own_filters
    filter_order = one_hot_rows(kind * filters + owner * own_filters + own)
    fft_size = 2 * tokens
    outer = fft_size // LANES
    used = outer // 2
    angle = 2.0 * math.pi * (np.outer(np.arange(outer), np.arange(used)) % outer) / outer
    cosine, sine = np.cos(angle), np.sin(angle)
    first = np.block([[cosine, sine], [-sine, cosine]])
    high, low = host_split(first)
    first_cat = np.concatenate([high, low, high], axis=1)
    high, low = high[:, :used], low[:, :used]
    first_real = np.concatenate([high, low, high], axis=1)
    last = np.block([[cosine.T, -sine.T], [sine.T, cosine.T]]) / fft_size
    high, low = host_split(last)
    last_cat = np.concatenate([high, low, high], axis=1)
    angle = 2.0 * math.pi * (np.outer(np.arange(LANES), np.arange(LANES)) % LANES) / LANES
    cosine, sine = np.cos(angle), np.sin(angle)
    inner = np.stack(host_split(np.block([[cosine, -sine], [sine, cosine]])))
    inner_back = np.stack(host_split(np.block([[cosine, sine], [-sine, cosine]])))
    angle = -2.0 * math.pi * np.outer(np.arange(outer), np.arange(LANES)) / fft_size
    twiddles = np.stack([np.cos(angle), np.sin(angle)]).astype(np.float32)
    return (
        order,
        np.ascontiguousarray(order.T),
        filter_order,
        np.ascontiguousarray(filter_order.T),
        first_cat,
        first_real,
        last_cat,
        inner,
        inner_back,
        twiddles,
    )


def dot32(left, right):
    return jnp.dot(left, right, preferred_element_type=F32)


def inner_product(value, table_ref):
    high, low = split16(value)
    return dot32(high, table_ref[0]) + dot32(low, table_ref[0]) + dot32(high, table_ref[1])


def outer_product(table, value):
    high, low = split16(value)
    return dot32(table, jnp.concatenate([high, high, low], axis=0))


def halves_of(value):
    return value[:, :LANES], value[:, LANES:]


def product(first, second, conjugate):
    a, b = halves_of(first)
    c, d = halves_of(second)
    if conjugate:
        return jnp.concatenate([a * c + b * d, b * c - a * d], axis=1)
    return jnp.concatenate([a * c - b * d, a * d + b * c], axis=1)


def delayed(value, by):
    if by == 0:
        return value
    zeros = jnp.zeros((value.shape[0], LANES), F32)
    return pltpu.roll(jnp.concatenate([zeros, value], axis=1), by, 1)[:, LANES:]


def advanced(value, by):
    if by == 0:
        return value
    length = value.shape[1]
    zeros = jnp.zeros((value.shape[0], LANES), F32)
    return pltpu.roll(jnp.concatenate([value, zeros], axis=1), length + LANES - by, 1)[:, :length]


def kernel(
    filter_scale,
    streams,
    out_grad,
    long_filter,
    short_filters,
    skip_gain,
    order,
    order_t,
    filter_order,
    filter_order_t,
    first_cat,
    first_real,
    last_cat,
    inner,
    inner_back,
    twiddles,
    stream_grad,
    filter_grad,
    sent,
    held,
    answers,
    results,
    signal_rows,
    filter_rows,
    own_part,
    other_part,
    send_sem,
    recv_sem,
    back_send_sem,
    back_recv_sem,
    part_sem,
):
    devices = sent.shape[0]
    rows = sent.shape[1]
    length = streams.shape[2]
    filters = long_filter.shape[0]
    taps = short_filters.shape[1]
    own_filters = filters // devices
    members = rows // own_filters
    pairs = rows // 2
    per_filter = members // 2
    used = devices * length // LANES
    outer = 2 * used
    pieces = length // LANES
    me = lax.axis_index("seq")
    other = 1 - lax.axis_index("chan")

    barrier = pltpu.get_barrier_semaphore()
    for step in range(1, devices):
        pl.semaphore_signal(
            barrier, inc=1, device_id={"seq": lax.rem(me + step, devices)}, device_id_type=MESH
        )
    pl.semaphore_signal(barrier, inc=1, device_id={"chan": other}, device_id_type=MESH)

    for index in range(4):
        block = out_grad[...] if index == 3 else streams[index]
        moved = dot32(order[...], block).astype(BF16)
        sent[:, :, index * length : (index + 1) * length] = moved.reshape(devices, rows, length)
    high, low = split16(long_filter[...])
    stacked = []
    for piece in range(pieces):
        columns = slice(piece * LANES, (piece + 1) * LANES)
        stacked += [high[:, columns], low[:, columns]]
    moved = dot32(filter_order[...], jnp.concatenate(stacked, axis=0)).astype(BF16)
    sent[:, :, 4 * length :] = moved.reshape(devices, rows, LANES)

    pl.semaphore_wait(barrier, devices)

    def exchange(source, target, send, recv):
        copies = []
        for step in range(1, devices):
            peer = lax.rem(me + step, devices)
            copy = pltpu.make_async_remote_copy(
                src_ref=source.at[peer],
                dst_ref=target.at[me],
                send_sem=send.at[peer],
                recv_sem=recv.at[me],
                device_id={"seq": peer},
                device_id_type=MESH,
            )
            copy.start()
            copies.append(copy)
        target[me] = source[me]
        return copies

    def finish(copies, source, target, send, recv):
        for step in range(1, devices):
            peer = lax.rem(me + step, devices)
            pltpu.make_async_remote_copy(
                src_ref=source.at[peer],
                dst_ref=target.at[peer],
                send_sem=send.at[peer],
                recv_sem=recv.at[peer],
                device_id={"seq": peer},
                device_id_type=MESH,
            ).wait_recv()

    copies = exchange(sent, held, send_sem, recv_sem)
    picked = order[pl.ds(pl.multiple_of(me * rows, rows), rows), :].astype(F32)

    def own_columns(values):
        return lax.dot_general(
            picked,
            values,
            (((1,), (1,)), ((), ())),
            precision=lax.Precision.HIGHEST,
            preferred_element_type=F32,
        )

    weights = [own_columns(short_filters[index]) for index in range(3)]
    gain = jnp.sum(picked * skip_gain[...], axis=1, keepdims=True)
    finish(copies, sent, held, send_sem, recv_sem)

    def whole(index):
        columns = slice(index * length, (index + 1) * length)
        return jnp.concatenate(
            [held[source, :, columns].astype(F32) for source in range(devices)], axis=1
        )

    filtered = []
    for index in range(3):
        value = whole(index)
        total = weights[index][:, 0:1] * value
        for offset in range(1, taps):
            total = total + weights[index][:, offset : offset + 1] * delayed(value, offset)
        filtered.append(total)
    out_float = whole(3)
    gated_prod = filtered[1] * filtered[2]
    gate_grad = out_float * filtered[0]
    for block in range(used):
        columns = slice(block * LANES, (block + 1) * LANES)
        signal_rows[0, block * rows : (block + 1) * rows, :] = gated_prod[:, columns]
        signal_rows[1, block * rows : (block + 1) * rows, :] = gate_grad[:, columns]
    for source in range(devices):
        filter_rows[source * rows : (source + 1) * rows, :] = held[source, :, 4 * length :].astype(
            F32
        )

    def channel_rows(which, channel):
        return signal_rows[which, pl.ds(channel, used, stride=rows), :]

    stride = 2 * own_filters

    def filter_part(part):
        return jnp.concatenate(
            [
                filter_rows[pl.ds(part * own_filters + own, used, stride=stride), :]
                for own in range(own_filters)
            ],
            axis=1,
        ).astype(BF16)

    def packed(which, part):
        return [channel_rows(which, 2 * pair + part) for pair in range(pairs)]

    signals = jnp.concatenate(
        [
            jnp.concatenate(packed(0, part) + packed(1, part), axis=1)
            for part in range(2)
        ],
        axis=0,
    )
    part_high, part_low = filter_part(0), filter_part(1)
    outer_out = jnp.concatenate(
        [
            outer_product(first_cat[...], signals),
            dot32(first_real[...], jnp.concatenate([part_high, part_high, part_low], axis=0)),
        ],
        axis=1,
    )
    twiddle_re, twiddle_im = twiddles[0], twiddles[1]
    count = 2 * pairs + own_filters
    turned = []
    for index in range(count):
        columns = slice(index * LANES, (index + 1) * LANES)
        real_part, imag_part = outer_out[:outer, columns], outer_out[outer:, columns]
        turned.append(
            jnp.concatenate(
                [
                    real_part * twiddle_re - imag_part * twiddle_im,
                    real_part * twiddle_im + imag_part * twiddle_re,
                ],
                axis=1,
            )
        )
    spectra = inner_product(jnp.concatenate(turned, axis=0), inner)

    def spectrum(index):
        return spectra[index * outer : (index + 1) * outer]

    def inverse(values, table):
        inner_out = inner_product(jnp.concatenate(values, axis=0), inner_back)
        columns = []
        for index in range(len(values)):
            real_part, imag_part = halves_of(inner_out[index * outer : (index + 1) * outer])
            columns.append(
                jnp.concatenate(
                    [
                        real_part * twiddle_re + imag_part * twiddle_im,
                        imag_part * twiddle_re - real_part * twiddle_im,
                    ],
                    axis=0,
                )
            )
        return outer_product(table, jnp.concatenate(columns, axis=1))

    sums = []
    for own in range(own_filters):
        total = None
        for index in range(own * per_filter, (own + 1) * per_filter):
            term = product(spectrum(pairs + index), spectrum(index), True)
            total = term if total is None else total + term
        sums.append(total)
    own_part[...] = inverse(sums, last_cat[:used, :])
    part_copy = pltpu.make_async_remote_copy(
        src_ref=own_part,
        dst_ref=other_part,
        send_sem=part_sem.at[0],
        recv_sem=part_sem.at[1],
        device_id={"chan": other},
        device_id_type=MESH,
    )
    part_copy.start()

    products = []
    for index in range(2 * pairs):
        filter_spec = spectrum(2 * pairs + index % pairs // per_filter)
        products.append(product(spectrum(index), filter_spec, index >= pairs))
    times = inverse(products, last_cat[...])
    for index in range(2 * pairs):
        which, pair = index // pairs, index % pairs
        columns = slice(index * LANES, (index + 1) * LANES)
        for part in range(2):
            signal_rows[which, pl.ds(2 * pair + part, used, stride=rows), :] = times[
                part * used : (part + 1) * used, columns
            ]

    def joined(which):
        return jnp.concatenate(
            [signal_rows[which, block * rows : (block + 1) * rows, :] for block in range(used)],
            axis=1,
        )

    conv_out = joined(0) + gain * gated_prod
    gated_grad = joined(1) + gain * gate_grad
    grads = (out_float * conv_out, gated_grad * filtered[2], gated_grad * filtered[1])
    for index in range(3):
        value = grads[index]
        total = weights[index][:, 0:1] * value
        for offset in range(1, taps):
            total = total + weights[index][:, offset : offset + 1] * advanced(value, offset)
        total = total.astype(BF16)
        for target in range(devices):
            answers[target, :, index * length : (index + 1) * length] = total[
                :, target * length : (target + 1) * length
            ]

    part_copy.wait()
    high, low = split16((own_part[...] + other_part[...]) * filter_scale)
    for own in range(own_filters):
        columns = slice(own * LANES, (own + 1) * LANES)
        filter_rows[pl.ds(own, used, stride=stride), :] = high[:, columns].astype(F32)
        filter_rows[pl.ds(own_filters + own, used, stride=stride), :] = low[:, columns].astype(F32)
    for target in range(devices):
        answers[target, :, 3 * length :] = filter_rows[
            target * rows : (target + 1) * rows, :
        ].astype(BF16)

    back_copies = exchange(answers, results, back_send_sem, back_recv_sem)
    for copy in copies:
        copy.wait_send()
    finish(back_copies, answers, results, back_send_sem, back_recv_sem)
    for index in range(3):
        block = results[:, :, index * length : (index + 1) * length].reshape(devices * rows, length)
        stream_grad[index] = dot32(order_t[...], block).astype(BF16)
    block = results[:, :, 3 * length :].reshape(devices * rows, LANES)
    moved = dot32(filter_order_t[...], block)
    for piece in range(pieces):
        start = 2 * piece * filters
        filter_grad[:, piece * LANES : (piece + 1) * LANES] = (
            moved[start : start + filters] + moved[start + filters : start + 2 * filters]
        )
    for copy in back_copies:
        copy.wait_send()


def fast_local(streams, short_filters, long_filter, skip_gain, out_grad):
    devices = lax.axis_size("seq")
    channels, length = streams.shape[1:]
    filters = long_filter.shape[0]
    tokens = devices * length
    rows = channels // devices
    own_filters = filters // devices
    used = tokens // LANES
    members_total = channels * lax.axis_size("chan") // filters
    constants = [jnp.asarray(table) for table in tables(channels, filters, devices, tokens)]
    arguments = [
        streams,
        out_grad,
        long_filter,
        short_filters,
        skip_gain.reshape(1, channels),
    ] + constants
    vmem = pl.BlockSpec(memory_space=pltpu.VMEM)
    width = 4 * length + LANES
    width_back = 3 * length + LANES
    return pl.pallas_call(
        functools.partial(kernel, 1.0 / math.sqrt(members_total * tokens)),
        out_shape=(
            jax.ShapeDtypeStruct(streams.shape, BF16),
            jax.ShapeDtypeStruct(long_filter.shape, F32),
        ),
        in_specs=[vmem] * len(arguments),
        out_specs=(vmem, vmem),
        scratch_shapes=[
            pltpu.VMEM((devices, rows, width), BF16),
            pltpu.VMEM((devices, rows, width), BF16),
            pltpu.VMEM((devices, rows, width_back), BF16),
            pltpu.VMEM((devices, rows, width_back), BF16),
            pltpu.VMEM((2, used * rows, LANES), F32),
            pltpu.VMEM((devices * rows, LANES), F32),
            pltpu.VMEM((used, own_filters * LANES), F32),
            pltpu.VMEM((used, own_filters * LANES), F32),
            pltpu.SemaphoreType.DMA((devices,)),
            pltpu.SemaphoreType.DMA((devices,)),
            pltpu.SemaphoreType.DMA((devices,)),
            pltpu.SemaphoreType.DMA((devices,)),
            pltpu.SemaphoreType.DMA((2,)),
        ],
        compiler_params=pltpu.CompilerParams(
            collective_id=0, has_side_effects=True, vmem_limit_bytes=48 * 2**20
        ),
    )(*arguments)


def fits_fast(mesh, channels, tokens, filters):
    devices, groups = mesh.shape["seq"], mesh.shape["chan"]
    channels, length = channels // groups, tokens // devices
    if groups != 2 or filters % devices or channels % (2 * filters) or channels % (16 * devices):
        return False
    return length == 2 * LANES and channels // devices == 4 * (filters // devices)


def solution(mesh):
    in_specs = (
        P(None, "chan", "seq"),
        P(None, None, "chan"),
        P(None, "seq"),
        P("chan"),
        P("chan", "seq"),
    )
    out_specs = (P(None, "chan", "seq"), P(None, "seq"))

    def whole_program(streams, short_filters, long_filter, skip_gain, out_grad):
        fast = fits_fast(mesh, streams.shape[1], streams.shape[2], long_filter.shape[0])
        return jax.shard_map(
            fast_local if fast else local,
            mesh=mesh,
            in_specs=in_specs,
            out_specs=out_specs,
            check_vma=False,
        )(streams, short_filters, long_filter, skip_gain, out_grad)

    return whole_program
```

```python
import functools
import math

import jax
import jax.numpy as jnp
import ml_dtypes
import numpy as np
from jax import lax
from jax.experimental import pallas as pl
from jax.experimental.pallas import tpu as pltpu
from jax.sharding import PartitionSpec as P

MESH = pl.DeviceIdType.MESH


def partner_2(value, axis, apart):
    mask = 2**apart
    pairs = [(source, source ^ mask) for source in range(lax.axis_size(axis))]
    return lax.ppermute(value, axis, pairs)


def shifted(shard, axis, by):
    length = lax.axis_size(axis)
    pairs = [(i, i + by) for i in range(length) if 0 <= i + by < length]
    return lax.ppermute(shard, axis, pairs)


def rotate(real_part, imag_part, cosine, sine_part):
    return (real_part * cosine - imag_part * sine_part, real_part * sine_part + imag_part * cosine)


def split_halves(signal):
    middle = signal.shape[-1] // 2
    return (signal[..., :middle], signal[..., middle:])


def join_halves(real_part, imag_part):
    return jnp.concatenate([real_part, imag_part], axis=-1)


def complex_product(first_op, second_op, conjugate):
    first_re, first_im = split_halves(first_op)
    second_re, second_im = split_halves(second_op)
    if conjugate:
        second_im = -second_im
    return join_halves(
        first_re * second_re - first_im * second_im, first_re * second_im + first_im * second_re
    )


def dft_table(length, direction, scaling):
    indices = jnp.arange(length, dtype=jnp.int32)
    phases = (indices[:, None] * indices[None, :] % length).astype(jnp.float32) * (
        direction * 2.0 * math.pi / length
    )
    cosine = jnp.cos(phases) * scaling
    sine_part = jnp.sin(phases) * scaling
    upper_rows = jnp.concatenate([cosine, sine_part], axis=1)
    lower_rows = jnp.concatenate([-sine_part, cosine], axis=1)
    return jnp.concatenate([upper_rows, lower_rows], axis=0)


def section_count():
    return lax.axis_size("seq").bit_length() - 1


def bit_reverse(position, sections):
    result = jnp.zeros((), jnp.int32)
    for bit_level in range(sections):
        result = result + position // (1 << bit_level) % 2 * (1 << sections - 1 - bit_level)
    return result


def held_index():
    return bit_reverse(lax.axis_index("seq"), section_count())


def inner_twiddle(signal, held, direction):
    length = signal.shape[-1] // 2
    seq_total = length * lax.axis_size("seq")
    indices = jnp.arange(length, dtype=jnp.int32)
    phases = (indices * held % seq_total).astype(jnp.float32) * (
        direction * 2.0 * math.pi / seq_total
    )
    real_part, imag_part = split_halves(signal)
    turned_re, turned_im = rotate(real_part, imag_part, jnp.cos(phases), jnp.sin(phases))
    return join_halves(turned_re, turned_im)


def forward_sections(signal):
    position = lax.axis_index("seq")
    sections = section_count()
    for bit_level in reversed(range(sections)):
        half_span = 1 << bit_level
        partner = partner_2(signal, "seq", bit_level)
        upper_side = position // half_span % 2 == 1
        phases = (position % half_span).astype(jnp.float32) * (-math.pi / half_span)
        diff_re, diff_im = split_halves(partner - signal)
        turned_re, turned_im = rotate(diff_re, diff_im, jnp.cos(phases), jnp.sin(phases))
        signal = jnp.where(upper_side, join_halves(turned_re, turned_im), signal + partner)
    return signal


def inverse_sections(signal):
    position = lax.axis_index("seq")
    sections = section_count()
    for bit_level in range(sections):
        half_span = 1 << bit_level
        partner = partner_2(signal, "seq", bit_level)
        upper_side = position // half_span % 2 == 1
        phases = (position % half_span).astype(jnp.float32) * (math.pi / half_span)
        source = jnp.where(upper_side, signal, partner)
        base_term = jnp.where(upper_side, partner, signal)
        source_re, source_im = split_halves(source)
        turned_re, turned_im = rotate(source_re, source_im, jnp.cos(phases), jnp.sin(phases))
        turned = join_halves(turned_re, turned_im)
        signal = 0.5 * jnp.where(upper_side, base_term - turned, base_term + turned)
    return signal


def forward_dft(signal, dft_matrix):
    signal = forward_sections(signal)
    signal = inner_twiddle(signal, held_index(), -1.0)
    return jnp.dot(
        signal, dft_matrix, precision=lax.Precision.HIGHEST, preferred_element_type=jnp.float32
    )


def inverse_dft(spectra, dft_matrix):
    signal = jnp.dot(
        spectra, dft_matrix, precision=lax.Precision.HIGHEST, preferred_element_type=jnp.float32
    )
    signal = inner_twiddle(signal, held_index(), 1.0)
    return inverse_sections(signal)


def local(streams, short_filters, long_filter, skip_gain, out_grad):
    tap_count = short_filters.shape[1]
    reach_back = tap_count - 1
    channels_dev = streams.shape[1]
    length = streams.shape[2]
    filters = long_filter.shape[0]
    members = channels_dev // filters
    devices = lax.axis_size("seq")
    position = lax.axis_index("seq")
    seq_total = length * devices
    preceding = shifted(streams[:, :, length - reach_back :], "seq", 1)
    extended = jnp.concatenate([preceding, streams], axis=2).astype(jnp.float32)
    filtered = jnp.zeros(streams.shape, jnp.float32)
    for offset in range(tap_count):
        filtered = (
            filtered
            + short_filters[:, offset, :, None]
            * extended[:, :, reach_back - offset : reach_back - offset + length]
        )
    gate_out = filtered[0]
    gate_in = filtered[1]
    values = filtered[2]
    gated_prod = gate_in * values
    out_float = out_grad.astype(jnp.float32)
    gate_grad = out_float * gate_out
    signals = jnp.concatenate([gated_prod, gate_grad, long_filter], axis=0)
    twist_phase = (position * length + jnp.arange(length, dtype=jnp.int32)).astype(jnp.float32) * (
        -math.pi / seq_total
    )
    twist_re = jnp.cos(twist_phase)
    twist_im = jnp.sin(twist_phase)
    even_part = join_halves(signals, jnp.zeros_like(signals))
    odd_part = join_halves(signals * twist_re, signals * twist_im)
    spectra = forward_dft(
        jnp.concatenate([even_part, odd_part], axis=0), dft_table(length, -1.0, 1.0)
    )
    row_count = signals.shape[0]
    halves = (spectra[:row_count], spectra[row_count:])
    filter_specs = (halves[0][2 * channels_dev :], halves[1][2 * channels_dev :])
    products = []
    for half_index in range(2):
        part_spec = halves[half_index]
        gated_spec = part_spec[:channels_dev]
        grad_spec = part_spec[channels_dev : 2 * channels_dev]
        wide_filter = jnp.tile(filter_specs[half_index], (members, 1))
        products.append(complex_product(gated_spec, wide_filter, False))
        products.append(complex_product(grad_spec, wide_filter, True))
        products.append(
            complex_product(grad_spec, gated_spec, True)
            .reshape(members, filters, 2 * length)
            .sum(axis=0)
        )
    time_rows = inverse_dft(jnp.concatenate(products, axis=0), dft_table(length, 1.0, 1.0 / length))
    part_rows = 2 * channels_dev + filters
    even_re, even_im = split_halves(time_rows[:part_rows])
    odd_re, odd_im = split_halves(time_rows[part_rows:])
    combined = 0.5 * (even_re + twist_re * odd_re + twist_im * odd_im)
    conv_part = combined[:channels_dev]
    corr_part = combined[channels_dev : 2 * channels_dev]
    filter_local = combined[2 * channels_dev :]
    conv_out = conv_part + skip_gain[:, None] * gated_prod
    gated_grad = corr_part + skip_gain[:, None] * gate_grad
    members_total = channels_dev * lax.axis_size("chan") // filters
    filter_grad = lax.psum(filter_local, "chan") * (1.0 / math.sqrt(members_total * seq_total))
    grads_in = jnp.stack([out_float * conv_out, gated_grad * values, gated_grad * gate_in])
    following = shifted(grads_in[:, :, :reach_back], "seq", -1)
    extended_grad = jnp.concatenate([grads_in, following], axis=2)
    result = jnp.zeros(grads_in.shape, jnp.float32)
    for offset in range(tap_count):
        result = (
            result
            + short_filters[:, offset, :, None] * extended_grad[:, :, offset : offset + length]
        )
    return (result.astype(jnp.bfloat16), filter_grad)


BF16 = jnp.bfloat16
F32 = jnp.float32
LANES = 128
OPERANDS = 15


def split16(value):
    high = value.astype(BF16)
    return high, (value - high.astype(F32)).astype(BF16)


def host_split(table):
    high = table.astype(np.float32).astype(ml_dtypes.bfloat16)
    low = (table - high.astype(np.float64)).astype(np.float32).astype(ml_dtypes.bfloat16)
    return high, low


def one_hot_rows(sources):
    table = np.zeros((len(sources), len(sources)), np.float32)
    table[np.arange(len(sources)), sources] = 1.0
    return table.astype(ml_dtypes.bfloat16)


def tables(channels, filters, devices, tokens):
    members = channels // filters
    own_filters = filters // devices
    rows = np.arange(channels)
    order = one_hot_rows(filters * (rows % members) + rows // members)
    rows = np.arange(4 * filters)
    owner, kind, own = rows // (4 * own_filters), rows // own_filters % 4, rows % own_filters
    filter_order = one_hot_rows(kind * filters + owner * own_filters + own)
    fft_size = 2 * tokens
    outer = fft_size // LANES
    used = outer // 2
    angle = 2.0 * math.pi * (np.outer(np.arange(outer), np.arange(used)) % outer) / outer
    cosine, sine = np.cos(angle), np.sin(angle)
    first = np.block([[cosine, sine], [-sine, cosine]])
    high, low = host_split(first)
    first_cat = np.concatenate([high, low, high], axis=1)
    high, low = high[:, :used], low[:, :used]
    first_real = np.concatenate([high, low, high], axis=1)
    last = np.block([[cosine.T, -sine.T], [sine.T, cosine.T]]) / fft_size
    high, low = host_split(last)
    last_cat = np.concatenate([high, low, high], axis=1)
    angle = 2.0 * math.pi * (np.outer(np.arange(LANES), np.arange(LANES)) % LANES) / LANES
    cosine, sine = np.cos(angle), np.sin(angle)
    inner = np.stack(host_split(np.block([[cosine, -sine], [sine, cosine]])))
    inner_back = np.stack(host_split(np.block([[cosine, sine], [-sine, cosine]])))
    angle = -2.0 * math.pi * np.outer(np.arange(outer), np.arange(LANES)) / fft_size
    twiddles = np.stack([np.cos(angle), np.sin(angle)]).astype(np.float32)
    return (
        order,
        np.ascontiguousarray(order.T),
        filter_order,
        np.ascontiguousarray(filter_order.T),
        first_cat,
        first_real,
        last_cat,
        inner,
        inner_back,
        twiddles,
    )


def dot32(left, right):
    return jnp.dot(left, right, preferred_element_type=F32)


def inner_product(value, table_ref):
    high, low = split16(value)
    return dot32(high, table_ref[0]) + dot32(low, table_ref[0]) + dot32(high, table_ref[1])


def outer_product(table, value):
    high, low = split16(value)
    return dot32(table, jnp.concatenate([high, high, low], axis=0))


def halves_of(value):
    return value[:, :LANES], value[:, LANES:]


def product(first, second, conjugate):
    a, b = halves_of(first)
    c, d = halves_of(second)
    if conjugate:
        return jnp.concatenate([a * c + b * d, b * c - a * d], axis=1)
    return jnp.concatenate([a * c - b * d, a * d + b * c], axis=1)


def delayed(value, by):
    if by == 0:
        return value
    zeros = jnp.zeros((value.shape[0], LANES), F32)
    return pltpu.roll(jnp.concatenate([zeros, value], axis=1), by, 1)[:, LANES:]


def advanced(value, by):
    if by == 0:
        return value
    length = value.shape[1]
    zeros = jnp.zeros((value.shape[0], LANES), F32)
    return pltpu.roll(jnp.concatenate([value, zeros], axis=1), length + LANES - by, 1)[:, :length]


def kernel(filter_scale, *refs):
    operands, refs = refs[:OPERANDS], refs[OPERANDS:]
    stream_grad, filter_grad = refs[:2]
    (
        streams,
        out_grad,
        long_filter,
        short_filters,
        skip_gain,
        order,
        order_t,
        filter_order,
        filter_order_t,
        first_cat,
        first_real,
        last_cat,
        inner,
        inner_back,
        twiddles,
    ) = locals_ = refs[2 : 2 + OPERANDS]
    (
        sent,
        held,
        answers,
        results,
        signal_rows,
        filter_rows,
        own_part,
        other_part,
        send_sem,
        recv_sem,
        back_send_sem,
        back_recv_sem,
        part_sem,
        load_sem,
    ) = refs[2 + OPERANDS :]
    devices = sent.shape[0]
    rows = sent.shape[1]
    length = streams.shape[2]
    filters = long_filter.shape[0]
    taps = short_filters.shape[1]
    own_filters = filters // devices
    members = rows // own_filters
    pairs = rows // 2
    per_filter = members // 2
    used = devices * length // LANES
    outer = 2 * used
    pieces = length // LANES
    me = lax.axis_index("seq")
    other = 1 - lax.axis_index("chan")

    barrier = pltpu.get_barrier_semaphore()
    for step in range(1, devices):
        pl.semaphore_signal(
            barrier, inc=1, device_id={"seq": lax.rem(me + step, devices)}, device_id_type=MESH
        )
    pl.semaphore_signal(barrier, inc=1, device_id={"chan": other}, device_id_type=MESH)

    loads = [
        pltpu.make_async_copy(operands[index], locals_[index], load_sem.at[index])
        for index in range(OPERANDS)
    ]
    first = (5, 0, 1, 7, 2)
    later = [index for index in range(OPERANDS) if index not in first]
    for index in first + tuple(later):
        loads[index].start()
    for index in first:
        loads[index].wait()

    for index in range(4):
        block = out_grad[...] if index == 3 else streams[index]
        moved = dot32(order[...], block).astype(BF16)
        sent[:, :, index * length : (index + 1) * length] = moved.reshape(devices, rows, length)
    high, low = split16(long_filter[...])
    stacked = []
    for piece in range(pieces):
        columns = slice(piece * LANES, (piece + 1) * LANES)
        stacked += [high[:, columns], low[:, columns]]
    moved = dot32(filter_order[...], jnp.concatenate(stacked, axis=0)).astype(BF16)
    sent[:, :, 4 * length :] = moved.reshape(devices, rows, LANES)

    pl.semaphore_wait(barrier, devices)

    def exchange(source, target, send, recv):
        copies = []
        for step in range(1, devices):
            peer = lax.rem(me + step, devices)
            copy = pltpu.make_async_remote_copy(
                src_ref=source.at[peer],
                dst_ref=target.at[me],
                send_sem=send.at[peer],
                recv_sem=recv.at[me],
                device_id={"seq": peer},
                device_id_type=MESH,
            )
            copy.start()
            copies.append(copy)
        target[me] = source[me]
        return copies

    def finish(copies, source, target, send, recv):
        for step in range(1, devices):
            peer = lax.rem(me + step, devices)
            pltpu.make_async_remote_copy(
                src_ref=source.at[peer],
                dst_ref=target.at[peer],
                send_sem=send.at[peer],
                recv_sem=recv.at[peer],
                device_id={"seq": peer},
                device_id_type=MESH,
            ).wait_recv()

    copies = exchange(sent, held, send_sem, recv_sem)
    for index in later:
        loads[index].wait()
    picked = order[pl.ds(pl.multiple_of(me * rows, rows), rows), :].astype(F32)

    def own_columns(values):
        return lax.dot_general(
            picked,
            values,
            (((1,), (1,)), ((), ())),
            precision=lax.Precision.HIGHEST,
            preferred_element_type=F32,
        )

    weights = [own_columns(short_filters[index]) for index in range(3)]
    gain = jnp.sum(picked * skip_gain[...], axis=1, keepdims=True)
    finish(copies, sent, held, send_sem, recv_sem)

    def whole(index):
        columns = slice(index * length, (index + 1) * length)
        return jnp.concatenate(
            [held[source, :, columns].astype(F32) for source in range(devices)], axis=1
        )

    filtered = []
    for index in range(3):
        value = whole(index)
        total = weights[index][:, 0:1] * value
        for offset in range(1, taps):
            total = total + weights[index][:, offset : offset + 1] * delayed(value, offset)
        filtered.append(total)
    out_float = whole(3)
    gated_prod = filtered[1] * filtered[2]
    gate_grad = out_float * filtered[0]
    for block in range(used):
        columns = slice(block * LANES, (block + 1) * LANES)
        signal_rows[0, block * rows : (block + 1) * rows, :] = gated_prod[:, columns]
        signal_rows[1, block * rows : (block + 1) * rows, :] = gate_grad[:, columns]
    for source in range(devices):
        filter_rows[source * rows : (source + 1) * rows, :] = held[source, :, 4 * length :].astype(
            F32
        )

    def channel_rows(which, channel):
        return signal_rows[which, pl.ds(channel, used, stride=rows), :]

    stride = 2 * own_filters

    def filter_part(part):
        return jnp.concatenate(
            [
                filter_rows[pl.ds(part * own_filters + own, used, stride=stride), :]
                for own in range(own_filters)
            ],
            axis=1,
        ).astype(BF16)

    def packed(which, part):
        return [channel_rows(which, 2 * pair + part) for pair in range(pairs)]

    signals = jnp.concatenate(
        [
            jnp.concatenate(packed(0, part) + packed(1, part), axis=1)
            for part in range(2)
        ],
        axis=0,
    )
    part_high, part_low = filter_part(0), filter_part(1)
    outer_out = jnp.concatenate(
        [
            outer_product(first_cat[...], signals),
            dot32(first_real[...], jnp.concatenate([part_high, part_high, part_low], axis=0)),
        ],
        axis=1,
    )
    twiddle_re, twiddle_im = twiddles[0], twiddles[1]
    count = 2 * pairs + own_filters
    turned = []
    for index in range(count):
        columns = slice(index * LANES, (index + 1) * LANES)
        real_part, imag_part = outer_out[:outer, columns], outer_out[outer:, columns]
        turned.append(
            jnp.concatenate(
                [
                    real_part * twiddle_re - imag_part * twiddle_im,
                    real_part * twiddle_im + imag_part * twiddle_re,
                ],
                axis=1,
            )
        )
    spectra = inner_product(jnp.concatenate(turned, axis=0), inner)

    def spectrum(index):
        return spectra[index * outer : (index + 1) * outer]

    def inverse(values, table):
        inner_out = inner_product(jnp.concatenate(values, axis=0), inner_back)
        columns = []
        for index in range(len(values)):
            real_part, imag_part = halves_of(inner_out[index * outer : (index + 1) * outer])
            columns.append(
                jnp.concatenate(
                    [
                        real_part * twiddle_re + imag_part * twiddle_im,
                        imag_part * twiddle_re - real_part * twiddle_im,
                    ],
                    axis=0,
                )
            )
        return outer_product(table, jnp.concatenate(columns, axis=1))

    sums = []
    for own in range(own_filters):
        total = None
        for index in range(own * per_filter, (own + 1) * per_filter):
            term = product(spectrum(pairs + index), spectrum(index), True)
            total = term if total is None else total + term
        sums.append(total)
    own_part[...] = inverse(sums, last_cat[:used, :])
    part_copy = pltpu.make_async_remote_copy(
        src_ref=own_part,
        dst_ref=other_part,
        send_sem=part_sem.at[0],
        recv_sem=part_sem.at[1],
        device_id={"chan": other},
        device_id_type=MESH,
    )
    part_copy.start()

    products = []
    for index in range(2 * pairs):
        filter_spec = spectrum(2 * pairs + index % pairs // per_filter)
        products.append(product(spectrum(index), filter_spec, index >= pairs))
    times = inverse(products, last_cat[...])
    for index in range(2 * pairs):
        which, pair = index // pairs, index % pairs
        columns = slice(index * LANES, (index + 1) * LANES)
        for part in range(2):
            signal_rows[which, pl.ds(2 * pair + part, used, stride=rows), :] = times[
                part * used : (part + 1) * used, columns
            ]

    def joined(which):
        return jnp.concatenate(
            [signal_rows[which, block * rows : (block + 1) * rows, :] for block in range(used)],
            axis=1,
        )

    conv_out = joined(0) + gain * gated_prod
    gated_grad = joined(1) + gain * gate_grad
    grads = (out_float * conv_out, gated_grad * filtered[2], gated_grad * filtered[1])
    for index in range(3):
        value = grads[index]
        total = weights[index][:, 0:1] * value
        for offset in range(1, taps):
            total = total + weights[index][:, offset : offset + 1] * advanced(value, offset)
        total = total.astype(BF16)
        for target in range(devices):
            answers[target, :, index * length : (index + 1) * length] = total[
                :, target * length : (target + 1) * length
            ]

    part_copy.wait()
    high, low = split16((own_part[...] + other_part[...]) * filter_scale)
    for own in range(own_filters):
        columns = slice(own * LANES, (own + 1) * LANES)
        filter_rows[pl.ds(own, used, stride=stride), :] = high[:, columns].astype(F32)
        filter_rows[pl.ds(own_filters + own, used, stride=stride), :] = low[:, columns].astype(F32)
    for target in range(devices):
        answers[target, :, 3 * length :] = filter_rows[
            target * rows : (target + 1) * rows, :
        ].astype(BF16)

    back_copies = exchange(answers, results, back_send_sem, back_recv_sem)
    for copy in copies:
        copy.wait_send()
    finish(back_copies, answers, results, back_send_sem, back_recv_sem)
    for index in range(3):
        block = results[:, :, index * length : (index + 1) * length].reshape(devices * rows, length)
        stream_grad[index] = dot32(order_t[...], block).astype(BF16)
    block = results[:, :, 3 * length :].reshape(devices * rows, LANES)
    moved = dot32(filter_order_t[...], block)
    for piece in range(pieces):
        start = 2 * piece * filters
        filter_grad[:, piece * LANES : (piece + 1) * LANES] = (
            moved[start : start + filters] + moved[start + filters : start + 2 * filters]
        )
    for copy in back_copies:
        copy.wait_send()


def fast_local(streams, short_filters, long_filter, skip_gain, out_grad):
    devices = lax.axis_size("seq")
    channels, length = streams.shape[1:]
    filters = long_filter.shape[0]
    tokens = devices * length
    rows = channels // devices
    own_filters = filters // devices
    used = tokens // LANES
    members_total = channels * lax.axis_size("chan") // filters
    constants = [jnp.asarray(table) for table in tables(channels, filters, devices, tokens)]
    arguments = [
        streams,
        out_grad,
        long_filter,
        short_filters,
        skip_gain.reshape(1, channels),
    ] + constants
    vmem = pl.BlockSpec(memory_space=pltpu.VMEM)
    width = 4 * length + LANES
    width_back = 3 * length + LANES
    return pl.pallas_call(
        functools.partial(kernel, 1.0 / math.sqrt(members_total * tokens)),
        out_shape=(
            jax.ShapeDtypeStruct(streams.shape, BF16),
            jax.ShapeDtypeStruct(long_filter.shape, F32),
        ),
        in_specs=[pl.BlockSpec(memory_space=pltpu.HBM)] * len(arguments),
        out_specs=(vmem, vmem),
        scratch_shapes=[pltpu.VMEM(value.shape, value.dtype) for value in arguments]
        + [
            pltpu.VMEM((devices, rows, width), BF16),
            pltpu.VMEM((devices, rows, width), BF16),
            pltpu.VMEM((devices, rows, width_back), BF16),
            pltpu.VMEM((devices, rows, width_back), BF16),
            pltpu.VMEM((2, used * rows, LANES), F32),
            pltpu.VMEM((devices * rows, LANES), F32),
            pltpu.VMEM((used, own_filters * LANES), F32),
            pltpu.VMEM((used, own_filters * LANES), F32),
            pltpu.SemaphoreType.DMA((devices,)),
            pltpu.SemaphoreType.DMA((devices,)),
            pltpu.SemaphoreType.DMA((devices,)),
            pltpu.SemaphoreType.DMA((devices,)),
            pltpu.SemaphoreType.DMA((2,)),
            pltpu.SemaphoreType.DMA((OPERANDS,)),
        ],
        compiler_params=pltpu.CompilerParams(
            collective_id=0, has_side_effects=True, vmem_limit_bytes=62 * 2**20
        ),
    )(*arguments)


def fits_fast(mesh, channels, tokens, filters):
    devices, groups = mesh.shape["seq"], mesh.shape["chan"]
    channels, length = channels // groups, tokens // devices
    if groups != 2 or filters % devices or channels % (2 * filters) or channels % (16 * devices):
        return False
    return length == 2 * LANES and channels // devices == 4 * (filters // devices)


def solution(mesh):
    in_specs = (
        P(None, "chan", "seq"),
        P(None, None, "chan"),
        P(None, "seq"),
        P("chan"),
        P("chan", "seq"),
    )
    out_specs = (P(None, "chan", "seq"), P(None, "seq"))

    def whole_program(streams, short_filters, long_filter, skip_gain, out_grad):
        fast = fits_fast(mesh, streams.shape[1], streams.shape[2], long_filter.shape[0])
        return jax.shard_map(
            fast_local if fast else local,
            mesh=mesh,
            in_specs=in_specs,
            out_specs=out_specs,
            check_vma=False,
        )(streams, short_filters, long_filter, skip_gain, out_grad)

    return whole_program
```

```python
import functools
import math

import jax
import jax.numpy as jnp
import ml_dtypes
import numpy as np
from jax import lax
from jax.experimental import pallas as pl
from jax.experimental.pallas import tpu as pltpu
from jax.sharding import PartitionSpec as P

MESH = pl.DeviceIdType.MESH


def partner_2(value, axis, apart):
    mask = 2**apart
    pairs = [(source, source ^ mask) for source in range(lax.axis_size(axis))]
    return lax.ppermute(value, axis, pairs)


def shifted(shard, axis, by):
    length = lax.axis_size(axis)
    pairs = [(i, i + by) for i in range(length) if 0 <= i + by < length]
    return lax.ppermute(shard, axis, pairs)


def rotate(real_part, imag_part, cosine, sine_part):
    return (real_part * cosine - imag_part * sine_part, real_part * sine_part + imag_part * cosine)


def split_halves(signal):
    middle = signal.shape[-1] // 2
    return (signal[..., :middle], signal[..., middle:])


def join_halves(real_part, imag_part):
    return jnp.concatenate([real_part, imag_part], axis=-1)


def complex_product(first_op, second_op, conjugate):
    first_re, first_im = split_halves(first_op)
    second_re, second_im = split_halves(second_op)
    if conjugate:
        second_im = -second_im
    return join_halves(
        first_re * second_re - first_im * second_im, first_re * second_im + first_im * second_re
    )


def dft_table(length, direction, scaling):
    indices = jnp.arange(length, dtype=jnp.int32)
    phases = (indices[:, None] * indices[None, :] % length).astype(jnp.float32) * (
        direction * 2.0 * math.pi / length
    )
    cosine = jnp.cos(phases) * scaling
    sine_part = jnp.sin(phases) * scaling
    upper_rows = jnp.concatenate([cosine, sine_part], axis=1)
    lower_rows = jnp.concatenate([-sine_part, cosine], axis=1)
    return jnp.concatenate([upper_rows, lower_rows], axis=0)


def section_count():
    return lax.axis_size("seq").bit_length() - 1


def bit_reverse(position, sections):
    result = jnp.zeros((), jnp.int32)
    for bit_level in range(sections):
        result = result + position // (1 << bit_level) % 2 * (1 << sections - 1 - bit_level)
    return result


def held_index():
    return bit_reverse(lax.axis_index("seq"), section_count())


def inner_twiddle(signal, held, direction):
    length = signal.shape[-1] // 2
    seq_total = length * lax.axis_size("seq")
    indices = jnp.arange(length, dtype=jnp.int32)
    phases = (indices * held % seq_total).astype(jnp.float32) * (
        direction * 2.0 * math.pi / seq_total
    )
    real_part, imag_part = split_halves(signal)
    turned_re, turned_im = rotate(real_part, imag_part, jnp.cos(phases), jnp.sin(phases))
    return join_halves(turned_re, turned_im)


def forward_sections(signal):
    position = lax.axis_index("seq")
    sections = section_count()
    for bit_level in reversed(range(sections)):
        half_span = 1 << bit_level
        partner = partner_2(signal, "seq", bit_level)
        upper_side = position // half_span % 2 == 1
        phases = (position % half_span).astype(jnp.float32) * (-math.pi / half_span)
        diff_re, diff_im = split_halves(partner - signal)
        turned_re, turned_im = rotate(diff_re, diff_im, jnp.cos(phases), jnp.sin(phases))
        signal = jnp.where(upper_side, join_halves(turned_re, turned_im), signal + partner)
    return signal


def inverse_sections(signal):
    position = lax.axis_index("seq")
    sections = section_count()
    for bit_level in range(sections):
        half_span = 1 << bit_level
        partner = partner_2(signal, "seq", bit_level)
        upper_side = position // half_span % 2 == 1
        phases = (position % half_span).astype(jnp.float32) * (math.pi / half_span)
        source = jnp.where(upper_side, signal, partner)
        base_term = jnp.where(upper_side, partner, signal)
        source_re, source_im = split_halves(source)
        turned_re, turned_im = rotate(source_re, source_im, jnp.cos(phases), jnp.sin(phases))
        turned = join_halves(turned_re, turned_im)
        signal = 0.5 * jnp.where(upper_side, base_term - turned, base_term + turned)
    return signal


def forward_dft(signal, dft_matrix):
    signal = forward_sections(signal)
    signal = inner_twiddle(signal, held_index(), -1.0)
    return jnp.dot(
        signal, dft_matrix, precision=lax.Precision.HIGHEST, preferred_element_type=jnp.float32
    )


def inverse_dft(spectra, dft_matrix):
    signal = jnp.dot(
        spectra, dft_matrix, precision=lax.Precision.HIGHEST, preferred_element_type=jnp.float32
    )
    signal = inner_twiddle(signal, held_index(), 1.0)
    return inverse_sections(signal)


def local(streams, short_filters, long_filter, skip_gain, out_grad):
    tap_count = short_filters.shape[1]
    reach_back = tap_count - 1
    channels_dev = streams.shape[1]
    length = streams.shape[2]
    filters = long_filter.shape[0]
    members = channels_dev // filters
    devices = lax.axis_size("seq")
    position = lax.axis_index("seq")
    seq_total = length * devices
    preceding = shifted(streams[:, :, length - reach_back :], "seq", 1)
    extended = jnp.concatenate([preceding, streams], axis=2).astype(jnp.float32)
    filtered = jnp.zeros(streams.shape, jnp.float32)
    for offset in range(tap_count):
        filtered = (
            filtered
            + short_filters[:, offset, :, None]
            * extended[:, :, reach_back - offset : reach_back - offset + length]
        )
    gate_out = filtered[0]
    gate_in = filtered[1]
    values = filtered[2]
    gated_prod = gate_in * values
    out_float = out_grad.astype(jnp.float32)
    gate_grad = out_float * gate_out
    signals = jnp.concatenate([gated_prod, gate_grad, long_filter], axis=0)
    twist_phase = (position * length + jnp.arange(length, dtype=jnp.int32)).astype(jnp.float32) * (
        -math.pi / seq_total
    )
    twist_re = jnp.cos(twist_phase)
    twist_im = jnp.sin(twist_phase)
    even_part = join_halves(signals, jnp.zeros_like(signals))
    odd_part = join_halves(signals * twist_re, signals * twist_im)
    spectra = forward_dft(
        jnp.concatenate([even_part, odd_part], axis=0), dft_table(length, -1.0, 1.0)
    )
    row_count = signals.shape[0]
    halves = (spectra[:row_count], spectra[row_count:])
    filter_specs = (halves[0][2 * channels_dev :], halves[1][2 * channels_dev :])
    products = []
    for half_index in range(2):
        part_spec = halves[half_index]
        gated_spec = part_spec[:channels_dev]
        grad_spec = part_spec[channels_dev : 2 * channels_dev]
        wide_filter = jnp.tile(filter_specs[half_index], (members, 1))
        products.append(complex_product(gated_spec, wide_filter, False))
        products.append(complex_product(grad_spec, wide_filter, True))
        products.append(
            complex_product(grad_spec, gated_spec, True)
            .reshape(members, filters, 2 * length)
            .sum(axis=0)
        )
    time_rows = inverse_dft(jnp.concatenate(products, axis=0), dft_table(length, 1.0, 1.0 / length))
    part_rows = 2 * channels_dev + filters
    even_re, even_im = split_halves(time_rows[:part_rows])
    odd_re, odd_im = split_halves(time_rows[part_rows:])
    combined = 0.5 * (even_re + twist_re * odd_re + twist_im * odd_im)
    conv_part = combined[:channels_dev]
    corr_part = combined[channels_dev : 2 * channels_dev]
    filter_local = combined[2 * channels_dev :]
    conv_out = conv_part + skip_gain[:, None] * gated_prod
    gated_grad = corr_part + skip_gain[:, None] * gate_grad
    members_total = channels_dev * lax.axis_size("chan") // filters
    filter_grad = lax.psum(filter_local, "chan") * (1.0 / math.sqrt(members_total * seq_total))
    grads_in = jnp.stack([out_float * conv_out, gated_grad * values, gated_grad * gate_in])
    following = shifted(grads_in[:, :, :reach_back], "seq", -1)
    extended_grad = jnp.concatenate([grads_in, following], axis=2)
    result = jnp.zeros(grads_in.shape, jnp.float32)
    for offset in range(tap_count):
        result = (
            result
            + short_filters[:, offset, :, None] * extended_grad[:, :, offset : offset + length]
        )
    return (result.astype(jnp.bfloat16), filter_grad)


BF16 = jnp.bfloat16
F32 = jnp.float32
LANES = 128
OPERANDS = 15


def split16(value):
    high = value.astype(BF16)
    return high, (value - high.astype(F32)).astype(BF16)


def host_split(table):
    high = table.astype(np.float32).astype(ml_dtypes.bfloat16)
    low = (table - high.astype(np.float64)).astype(np.float32).astype(ml_dtypes.bfloat16)
    return high, low


def one_hot_rows(sources):
    table = np.zeros((len(sources), len(sources)), np.float32)
    table[np.arange(len(sources)), sources] = 1.0
    return table.astype(ml_dtypes.bfloat16)


def tables(channels, filters, devices, tokens):
    members = channels // filters
    own_filters = filters // devices
    rows = np.arange(channels)
    block = channels // devices
    owner, side, within = rows // block, rows // (block // 2) % 2, rows % (block // 2)
    gather = np.zeros((2, channels, 2 * channels), np.float32)
    scatter = np.zeros((2, channels, 2 * channels), np.float32)
    for chunk in range(2):
        own = chunk * own_filters // 2 + within // members
        channel = filters * (within % members) + own_filters * owner + own
        gather[chunk, rows, side * channels + channel] = 1.0
        scatter[side, channel, chunk * channels + rows] = 1.0
    gather, scatter = gather.astype(ml_dtypes.bfloat16), scatter.astype(ml_dtypes.bfloat16)
    rows = np.arange(4 * filters)
    owner, kind, own = rows // (4 * own_filters), rows // own_filters % 4, rows % own_filters
    filter_order = one_hot_rows(kind * filters + owner * own_filters + own)
    fft_size = 2 * tokens
    outer = fft_size // LANES
    used = outer // 2
    angle = 2.0 * math.pi * (np.outer(np.arange(outer), np.arange(used)) % outer) / outer
    cosine, sine = np.cos(angle), np.sin(angle)
    first = np.block([[cosine, sine], [-sine, cosine]])
    high, low = host_split(first)
    first_cat = np.concatenate([high, low, high], axis=1)
    high, low = high[:, :used], low[:, :used]
    first_real = np.concatenate([high, low, high], axis=1)
    last = np.block([[cosine.T, -sine.T], [sine.T, cosine.T]]) / fft_size
    high, low = host_split(last)
    last_cat = np.concatenate([high, low, high], axis=1)
    angle = 2.0 * math.pi * (np.outer(np.arange(LANES), np.arange(LANES)) % LANES) / LANES
    cosine, sine = np.cos(angle), np.sin(angle)
    inner = np.stack(host_split(np.block([[cosine, -sine], [sine, cosine]])))
    inner_back = np.stack(host_split(np.block([[cosine, sine], [-sine, cosine]])))
    angle = -2.0 * math.pi * np.outer(np.arange(outer), np.arange(LANES)) / fft_size
    twiddles = np.stack([np.cos(angle), np.sin(angle)]).astype(np.float32)
    return (
        gather,
        scatter,
        filter_order,
        np.ascontiguousarray(filter_order.T),
        first_cat,
        first_real,
        last_cat,
        inner,
        inner_back,
        twiddles,
    )


def dot32(left, right):
    return jnp.dot(left, right, preferred_element_type=F32)


def inner_product(value, table_ref):
    high, low = split16(value)
    return dot32(high, table_ref[0]) + dot32(low, table_ref[0]) + dot32(high, table_ref[1])


def outer_product(table, value):
    high, low = split16(value)
    return dot32(table, jnp.concatenate([high, high, low], axis=0))


def halves_of(value):
    return value[:, :LANES], value[:, LANES:]


def product(first, second, conjugate):
    a, b = halves_of(first)
    c, d = halves_of(second)
    if conjugate:
        return jnp.concatenate([a * c + b * d, b * c - a * d], axis=1)
    return jnp.concatenate([a * c - b * d, a * d + b * c], axis=1)


def delayed(value, by):
    if by == 0:
        return value
    zeros = jnp.zeros((value.shape[0], LANES), F32)
    return pltpu.roll(jnp.concatenate([zeros, value], axis=1), by, 1)[:, LANES:]


def advanced(value, by):
    if by == 0:
        return value
    length = value.shape[1]
    zeros = jnp.zeros((value.shape[0], LANES), F32)
    return pltpu.roll(jnp.concatenate([value, zeros], axis=1), length + LANES - by, 1)[:, :length]


def kernel(filter_scale, *refs):
    operands, refs = refs[:OPERANDS], refs[OPERANDS:]
    stream_grad, filter_grad = refs[:2]
    (
        streams,
        out_grad,
        long_filter,
        short_filters,
        skip_gain,
        gather,
        scatter,
        filter_order,
        filter_order_t,
        first_cat,
        first_real,
        last_cat,
        inner,
        inner_back,
        twiddles,
    ) = locals_ = refs[2 : 2 + OPERANDS]
    (
        sent_zero,
        sent_one,
        held_zero,
        held_one,
        answers_zero,
        answers_one,
        results_zero,
        results_one,
        signal_rows,
        filter_rows,
        own_part,
        other_part,
        send_sem,
        recv_sem,
        back_send_sem,
        back_recv_sem,
        part_sem,
        load_sem,
    ) = refs[2 + OPERANDS :]
    devices = sent_one.shape[0]
    rows = sent_one.shape[1]
    half = rows // 2
    channels, length = streams.shape[1:]
    filters = long_filter.shape[0]
    taps = short_filters.shape[1]
    own_filters = filters // devices
    chunk_filters = own_filters // 2
    members = rows // own_filters
    pairs = half // 2
    per_filter = members // 2
    used = devices * length // LANES
    outer = 2 * used
    pieces = length // LANES
    sent, held = (sent_zero, sent_one), (held_zero, held_one)
    answers, results = (answers_zero, answers_one), (results_zero, results_one)
    me = lax.axis_index("seq")
    other = 1 - lax.axis_index("chan")

    barrier = pltpu.get_barrier_semaphore()
    for step in range(1, devices):
        pl.semaphore_signal(
            barrier, inc=1, device_id={"seq": lax.rem(me + step, devices)}, device_id_type=MESH
        )
    pl.semaphore_signal(barrier, inc=1, device_id={"chan": other}, device_id_type=MESH)

    loads = [
        pltpu.make_async_copy(operands[index], locals_[index], load_sem.at[index])
        for index in range(OPERANDS)
    ]
    first = (5, 0, 1, 7, 2)
    later = [index for index in range(OPERANDS) if index not in first]
    for index in first + tuple(later):
        loads[index].start()
    for index in first:
        loads[index].wait()

    blocks = (
        jnp.concatenate([streams[0], streams[2]], axis=0),
        jnp.concatenate([streams[1], out_grad[...]], axis=0),
    )

    def fill(chunk):
        for index in range(2):
            moved = dot32(gather[chunk], blocks[index]).astype(BF16)
            sent[chunk][:, :, index * length : (index + 1) * length] = moved.reshape(
                devices, rows, length
            )

    def exchange(source, target, send, recv, chunk):
        copies = []
        for step in range(1, devices):
            peer = lax.rem(me + step, devices)
            copy = pltpu.make_async_remote_copy(
                src_ref=source.at[peer],
                dst_ref=target.at[me],
                send_sem=send.at[chunk, peer],
                recv_sem=recv.at[chunk, me],
                device_id={"seq": peer},
                device_id_type=MESH,
            )
            copy.start()
            copies.append(copy)
        target[me] = source[me]
        return copies

    def finish(source, target, send, recv, chunk):
        for step in range(1, devices):
            peer = lax.rem(me + step, devices)
            pltpu.make_async_remote_copy(
                src_ref=source.at[peer],
                dst_ref=target.at[peer],
                send_sem=send.at[chunk, peer],
                recv_sem=recv.at[chunk, peer],
                device_id={"seq": peer},
                device_id_type=MESH,
            ).wait_recv()

    fill(0)
    high, low = split16(long_filter[...])
    stacked = []
    for piece in range(pieces):
        columns = slice(piece * LANES, (piece + 1) * LANES)
        stacked += [high[:, columns], low[:, columns]]
    moved = dot32(filter_order[...], jnp.concatenate(stacked, axis=0)).astype(BF16)
    sent_zero[:, :, 2 * length :] = moved.reshape(devices, rows, LANES)
    pl.semaphore_wait(barrier, devices)
    copies = exchange(sent_zero, held_zero, send_sem, recv_sem, 0)
    fill(1)
    copies += exchange(sent_one, held_one, send_sem, recv_sem, 1)

    for index in later:
        loads[index].wait()
    own_rows = pl.ds(pl.multiple_of(me * rows, rows), rows)
    picked = jnp.concatenate(
        [gather[chunk, own_rows, :channels].astype(F32)[:half] for chunk in range(2)], axis=0
    )

    def own_columns(values):
        return lax.dot_general(
            picked,
            values,
            (((1,), (1,)), ((), ())),
            precision=lax.Precision.HIGHEST,
            preferred_element_type=F32,
        )

    all_weights = [own_columns(short_filters[index]) for index in range(3)]
    all_gain = jnp.sum(picked * skip_gain[...], axis=1, keepdims=True)
    twiddle_re, twiddle_im = twiddles[0], twiddles[1]

    def forward(outer_out):
        turned = []
        for index in range(outer_out.shape[1] // LANES):
            columns = slice(index * LANES, (index + 1) * LANES)
            real_part, imag_part = outer_out[:outer, columns], outer_out[outer:, columns]
            turned.append(
                jnp.concatenate(
                    [
                        real_part * twiddle_re - imag_part * twiddle_im,
                        real_part * twiddle_im + imag_part * twiddle_re,
                    ],
                    axis=1,
                )
            )
        return inner_product(jnp.concatenate(turned, axis=0), inner)

    def spectrum(spectra, index):
        return spectra[index * outer : (index + 1) * outer]

    def inverse(values, table):
        inner_out = inner_product(jnp.concatenate(values, axis=0), inner_back)
        columns = []
        for index in range(len(values)):
            real_part, imag_part = halves_of(inner_out[index * outer : (index + 1) * outer])
            columns.append(
                jnp.concatenate(
                    [
                        real_part * twiddle_re + imag_part * twiddle_im,
                        imag_part * twiddle_re - real_part * twiddle_im,
                    ],
                    axis=0,
                )
            )
        return outer_product(table, jnp.concatenate(columns, axis=1))

    def filter_spectra():
        for source in range(devices):
            filter_rows[source * rows : (source + 1) * rows, :] = held_zero[
                source, :, 2 * length :
            ].astype(F32)
        high, low = [
            jnp.concatenate(
                [
                    filter_rows[pl.ds(part * own_filters + own, used, stride=stride), :]
                    for own in range(own_filters)
                ],
                axis=1,
            ).astype(BF16)
            for part in range(2)
        ]
        return forward(dot32(first_real[...], jnp.concatenate([high, high, low], axis=0)))

    stride = 2 * own_filters

    def work(chunk, filter_specs):
        weights = [value[chunk * half : (chunk + 1) * half] for value in all_weights]
        gain = all_gain[chunk * half : (chunk + 1) * half]
        received = held[chunk]

        def whole(side, index):
            columns = slice(index * length, (index + 1) * length)
            return jnp.concatenate(
                [
                    received[source, :, columns].astype(F32)[side * half : (side + 1) * half]
                    for source in range(devices)
                ],
                axis=1,
            )

        filtered = []
        for index, place in enumerate(((0, 0), (0, 1), (1, 0))):
            value = whole(*place)
            total = weights[index][:, 0:1] * value
            for offset in range(1, taps):
                total = total + weights[index][:, offset : offset + 1] * delayed(value, offset)
            filtered.append(total)
        out_float = whole(1, 1)
        gated_prod = filtered[1] * filtered[2]
        gate_grad = out_float * filtered[0]
        for block in range(used):
            columns = slice(block * LANES, (block + 1) * LANES)
            span = slice(block * half, (block + 1) * half)
            signal_rows[chunk, 0, span, :] = gated_prod[:, columns]
            signal_rows[chunk, 1, span, :] = gate_grad[:, columns]

        def packed(which, part):
            return [
                signal_rows[chunk, which, pl.ds(2 * pair + part, used, stride=half), :]
                for pair in range(pairs)
            ]

        signals = jnp.concatenate(
            [jnp.concatenate(packed(0, part) + packed(1, part), axis=1) for part in range(2)],
            axis=0,
        )
        spectra = forward(outer_product(first_cat[...], signals))
        sums = []
        for own in range(chunk_filters):
            total = None
            for index in range(own * per_filter, (own + 1) * per_filter):
                term = product(spectrum(spectra, pairs + index), spectrum(spectra, index), True)
                total = term if total is None else total + term
            sums.append(total)
        own_part[chunk] = inverse(sums, last_cat[:used, :])
        part_copy = pltpu.make_async_remote_copy(
            src_ref=own_part.at[chunk],
            dst_ref=other_part.at[chunk],
            send_sem=part_sem.at[0, chunk],
            recv_sem=part_sem.at[1, chunk],
            device_id={"chan": other},
            device_id_type=MESH,
        )
        part_copy.start()

        products = []
        for index in range(2 * pairs):
            own = chunk * chunk_filters + index % pairs // per_filter
            products.append(
                product(spectrum(spectra, index), spectrum(filter_specs, own), index >= pairs)
            )
        times = inverse(products, last_cat[...])
        for index in range(2 * pairs):
            which, pair = index // pairs, index % pairs
            columns = slice(index * LANES, (index + 1) * LANES)
            for part in range(2):
                signal_rows[chunk, which, pl.ds(2 * pair + part, used, stride=half), :] = times[
                    part * used : (part + 1) * used, columns
                ]

        def joined(which):
            return jnp.concatenate(
                [
                    signal_rows[chunk, which, block * half : (block + 1) * half, :]
                    for block in range(used)
                ],
                axis=1,
            )

        conv_out = joined(0) + gain * gated_prod
        gated_grad = joined(1) + gain * gate_grad
        grads = (out_float * conv_out, gated_grad * filtered[2], gated_grad * filtered[1])
        totals = []
        for index in range(3):
            value = grads[index]
            total = weights[index][:, 0:1] * value
            for offset in range(1, taps):
                total = total + weights[index][:, offset : offset + 1] * advanced(value, offset)
            totals.append(total)
        both = jnp.concatenate(totals[:2], axis=0).astype(BF16)
        for target in range(devices):
            start = target * length
            answers[chunk][target, :, :length] = both[:, start : start + length]
            answers[chunk][target, :, length : length + LANES] = jnp.concatenate(
                [
                    totals[2][:, start : start + LANES],
                    totals[2][:, start + LANES : start + 2 * LANES],
                ],
                axis=0,
            ).astype(BF16)
        return part_copy

    finish(sent_zero, held_zero, send_sem, recv_sem, 0)
    filter_specs = filter_spectra()
    part_copies = [work(0, filter_specs)]
    back_copies = exchange(answers_zero, results_zero, back_send_sem, back_recv_sem, 0)
    finish(sent_one, held_one, send_sem, recv_sem, 1)
    part_copies.append(work(1, filter_specs))

    for copy in part_copies:
        copy.wait()
    for chunk in range(2):
        high, low = split16((own_part[chunk] + other_part[chunk]) * filter_scale)
        for index in range(chunk_filters):
            columns = slice(index * LANES, (index + 1) * LANES)
            own = chunk * chunk_filters + index
            filter_rows[pl.ds(own, used, stride=stride), :] = high[:, columns].astype(F32)
            filter_rows[pl.ds(own_filters + own, used, stride=stride), :] = low[
                :, columns
            ].astype(F32)
    for target in range(devices):
        answers_one[target, :, length + LANES :] = filter_rows[
            target * rows : (target + 1) * rows, :
        ].astype(BF16)
    back_copies += exchange(answers_one, results_one, back_send_sem, back_recv_sem, 1)
    for copy in copies:
        copy.wait_send()
    for chunk in range(2):
        finish(answers[chunk], results[chunk], back_send_sem, back_recv_sem, chunk)

    def returned(columns):
        return jnp.concatenate(
            [results[chunk][:, :, columns].reshape(devices * rows, -1) for chunk in range(2)],
            axis=0,
        )

    for side in range(2):
        stream_grad[side] = dot32(scatter[side], returned(slice(0, length))).astype(BF16)
        stream_grad[2, :, side * LANES : (side + 1) * LANES] = dot32(
            scatter[side], returned(slice(length, length + LANES))
        ).astype(BF16)
    block = results_one[:, :, length + LANES :].reshape(devices * rows, LANES)
    moved = dot32(filter_order_t[...], block)
    for piece in range(pieces):
        start = 2 * piece * filters
        filter_grad[:, piece * LANES : (piece + 1) * LANES] = (
            moved[start : start + filters] + moved[start + filters : start + 2 * filters]
        )
    for copy in back_copies:
        copy.wait_send()


def fast_local(streams, short_filters, long_filter, skip_gain, out_grad):
    devices = lax.axis_size("seq")
    channels, length = streams.shape[1:]
    filters = long_filter.shape[0]
    tokens = devices * length
    rows = channels // devices
    own_filters = filters // devices
    used = tokens // LANES
    members_total = channels * lax.axis_size("chan") // filters
    constants = [jnp.asarray(table) for table in tables(channels, filters, devices, tokens)]
    arguments = [
        streams,
        out_grad,
        long_filter,
        short_filters,
        skip_gain.reshape(1, channels),
    ] + constants
    vmem = pl.BlockSpec(memory_space=pltpu.VMEM)
    return pl.pallas_call(
        functools.partial(kernel, 1.0 / math.sqrt(members_total * tokens)),
        out_shape=(
            jax.ShapeDtypeStruct(streams.shape, BF16),
            jax.ShapeDtypeStruct(long_filter.shape, F32),
        ),
        in_specs=[pl.BlockSpec(memory_space=pltpu.HBM)] * len(arguments),
        out_specs=(vmem, vmem),
        scratch_shapes=[pltpu.VMEM(value.shape, value.dtype) for value in arguments]
        + [
            pltpu.VMEM((devices, rows, 2 * length + LANES), BF16),
            pltpu.VMEM((devices, rows, 2 * length), BF16),
            pltpu.VMEM((devices, rows, 2 * length + LANES), BF16),
            pltpu.VMEM((devices, rows, 2 * length), BF16),
            pltpu.VMEM((devices, rows, length + LANES), BF16),
            pltpu.VMEM((devices, rows, length + 2 * LANES), BF16),
            pltpu.VMEM((devices, rows, length + LANES), BF16),
            pltpu.VMEM((devices, rows, length + 2 * LANES), BF16),
            pltpu.VMEM((2, 2, used * rows // 2, LANES), F32),
            pltpu.VMEM((devices * rows, LANES), F32),
            pltpu.VMEM((2, used, own_filters // 2 * LANES), F32),
            pltpu.VMEM((2, used, own_filters // 2 * LANES), F32),
            pltpu.SemaphoreType.DMA((2, devices)),
            pltpu.SemaphoreType.DMA((2, devices)),
            pltpu.SemaphoreType.DMA((2, devices)),
            pltpu.SemaphoreType.DMA((2, devices)),
            pltpu.SemaphoreType.DMA((2, 2)),
            pltpu.SemaphoreType.DMA((OPERANDS,)),
        ],
        compiler_params=pltpu.CompilerParams(
            collective_id=0, has_side_effects=True, vmem_limit_bytes=62 * 2**20
        ),
    )(*arguments)


def fits_fast(mesh, channels, tokens, filters):
    devices, groups = mesh.shape["seq"], mesh.shape["chan"]
    channels, length = channels // groups, tokens // devices
    if groups != 2 or filters % devices or channels % (2 * filters) or channels % (16 * devices):
        return False
    return length == 2 * LANES and channels // devices == 4 * (filters // devices) == 16


def solution(mesh):
    in_specs = (
        P(None, "chan", "seq"),
        P(None, None, "chan"),
        P(None, "seq"),
        P("chan"),
        P("chan", "seq"),
    )
    out_specs = (P(None, "chan", "seq"), P(None, "seq"))

    def whole_program(streams, short_filters, long_filter, skip_gain, out_grad):
        fast = fits_fast(mesh, streams.shape[1], streams.shape[2], long_filter.shape[0])
        return jax.shard_map(
            fast_local if fast else local,
            mesh=mesh,
            in_specs=in_specs,
            out_specs=out_specs,
            check_vma=False,
        )(streams, short_filters, long_filter, skip_gain, out_grad)

    return whole_program
```

```python
import functools
import math

import jax
import jax.numpy as jnp
import ml_dtypes
import numpy as np
from jax import lax
from jax.experimental import pallas as pl
from jax.experimental.pallas import tpu as pltpu
from jax.sharding import PartitionSpec as P

MESH = pl.DeviceIdType.MESH


def partner_2(value, axis, apart):
    mask = 2**apart
    pairs = [(source, source ^ mask) for source in range(lax.axis_size(axis))]
    return lax.ppermute(value, axis, pairs)


def shifted(shard, axis, by):
    length = lax.axis_size(axis)
    pairs = [(i, i + by) for i in range(length) if 0 <= i + by < length]
    return lax.ppermute(shard, axis, pairs)


def rotate(real_part, imag_part, cosine, sine_part):
    return (real_part * cosine - imag_part * sine_part, real_part * sine_part + imag_part * cosine)


def split_halves(signal):
    middle = signal.shape[-1] // 2
    return (signal[..., :middle], signal[..., middle:])


def join_halves(real_part, imag_part):
    return jnp.concatenate([real_part, imag_part], axis=-1)


def complex_product(first_op, second_op, conjugate):
    first_re, first_im = split_halves(first_op)
    second_re, second_im = split_halves(second_op)
    if conjugate:
        second_im = -second_im
    return join_halves(
        first_re * second_re - first_im * second_im, first_re * second_im + first_im * second_re
    )


def dft_table(length, direction, scaling):
    indices = jnp.arange(length, dtype=jnp.int32)
    phases = (indices[:, None] * indices[None, :] % length).astype(jnp.float32) * (
        direction * 2.0 * math.pi / length
    )
    cosine = jnp.cos(phases) * scaling
    sine_part = jnp.sin(phases) * scaling
    upper_rows = jnp.concatenate([cosine, sine_part], axis=1)
    lower_rows = jnp.concatenate([-sine_part, cosine], axis=1)
    return jnp.concatenate([upper_rows, lower_rows], axis=0)


def section_count():
    return lax.axis_size("seq").bit_length() - 1


def bit_reverse(position, sections):
    result = jnp.zeros((), jnp.int32)
    for bit_level in range(sections):
        result = result + position // (1 << bit_level) % 2 * (1 << sections - 1 - bit_level)
    return result


def held_index():
    return bit_reverse(lax.axis_index("seq"), section_count())


def inner_twiddle(signal, held, direction):
    length = signal.shape[-1] // 2
    seq_total = length * lax.axis_size("seq")
    indices = jnp.arange(length, dtype=jnp.int32)
    phases = (indices * held % seq_total).astype(jnp.float32) * (
        direction * 2.0 * math.pi / seq_total
    )
    real_part, imag_part = split_halves(signal)
    turned_re, turned_im = rotate(real_part, imag_part, jnp.cos(phases), jnp.sin(phases))
    return join_halves(turned_re, turned_im)


def forward_sections(signal):
    position = lax.axis_index("seq")
    sections = section_count()
    for bit_level in reversed(range(sections)):
        half_span = 1 << bit_level
        partner = partner_2(signal, "seq", bit_level)
        upper_side = position // half_span % 2 == 1
        phases = (position % half_span).astype(jnp.float32) * (-math.pi / half_span)
        diff_re, diff_im = split_halves(partner - signal)
        turned_re, turned_im = rotate(diff_re, diff_im, jnp.cos(phases), jnp.sin(phases))
        signal = jnp.where(upper_side, join_halves(turned_re, turned_im), signal + partner)
    return signal


def inverse_sections(signal):
    position = lax.axis_index("seq")
    sections = section_count()
    for bit_level in range(sections):
        half_span = 1 << bit_level
        partner = partner_2(signal, "seq", bit_level)
        upper_side = position // half_span % 2 == 1
        phases = (position % half_span).astype(jnp.float32) * (math.pi / half_span)
        source = jnp.where(upper_side, signal, partner)
        base_term = jnp.where(upper_side, partner, signal)
        source_re, source_im = split_halves(source)
        turned_re, turned_im = rotate(source_re, source_im, jnp.cos(phases), jnp.sin(phases))
        turned = join_halves(turned_re, turned_im)
        signal = 0.5 * jnp.where(upper_side, base_term - turned, base_term + turned)
    return signal


def forward_dft(signal, dft_matrix):
    signal = forward_sections(signal)
    signal = inner_twiddle(signal, held_index(), -1.0)
    return jnp.dot(
        signal, dft_matrix, precision=lax.Precision.HIGHEST, preferred_element_type=jnp.float32
    )


def inverse_dft(spectra, dft_matrix):
    signal = jnp.dot(
        spectra, dft_matrix, precision=lax.Precision.HIGHEST, preferred_element_type=jnp.float32
    )
    signal = inner_twiddle(signal, held_index(), 1.0)
    return inverse_sections(signal)


def local(streams, short_filters, long_filter, skip_gain, out_grad):
    tap_count = short_filters.shape[1]
    reach_back = tap_count - 1
    channels_dev = streams.shape[1]
    length = streams.shape[2]
    filters = long_filter.shape[0]
    members = channels_dev // filters
    devices = lax.axis_size("seq")
    position = lax.axis_index("seq")
    seq_total = length * devices
    preceding = shifted(streams[:, :, length - reach_back :], "seq", 1)
    extended = jnp.concatenate([preceding, streams], axis=2).astype(jnp.float32)
    filtered = jnp.zeros(streams.shape, jnp.float32)
    for offset in range(tap_count):
        filtered = (
            filtered
            + short_filters[:, offset, :, None]
            * extended[:, :, reach_back - offset : reach_back - offset + length]
        )
    gate_out = filtered[0]
    gate_in = filtered[1]
    values = filtered[2]
    gated_prod = gate_in * values
    out_float = out_grad.astype(jnp.float32)
    gate_grad = out_float * gate_out
    signals = jnp.concatenate([gated_prod, gate_grad, long_filter], axis=0)
    twist_phase = (position * length + jnp.arange(length, dtype=jnp.int32)).astype(jnp.float32) * (
        -math.pi / seq_total
    )
    twist_re = jnp.cos(twist_phase)
    twist_im = jnp.sin(twist_phase)
    even_part = join_halves(signals, jnp.zeros_like(signals))
    odd_part = join_halves(signals * twist_re, signals * twist_im)
    spectra = forward_dft(
        jnp.concatenate([even_part, odd_part], axis=0), dft_table(length, -1.0, 1.0)
    )
    row_count = signals.shape[0]
    halves = (spectra[:row_count], spectra[row_count:])
    filter_specs = (halves[0][2 * channels_dev :], halves[1][2 * channels_dev :])
    products = []
    for half_index in range(2):
        part_spec = halves[half_index]
        gated_spec = part_spec[:channels_dev]
        grad_spec = part_spec[channels_dev : 2 * channels_dev]
        wide_filter = jnp.tile(filter_specs[half_index], (members, 1))
        products.append(complex_product(gated_spec, wide_filter, False))
        products.append(complex_product(grad_spec, wide_filter, True))
        products.append(
            complex_product(grad_spec, gated_spec, True)
            .reshape(members, filters, 2 * length)
            .sum(axis=0)
        )
    time_rows = inverse_dft(jnp.concatenate(products, axis=0), dft_table(length, 1.0, 1.0 / length))
    part_rows = 2 * channels_dev + filters
    even_re, even_im = split_halves(time_rows[:part_rows])
    odd_re, odd_im = split_halves(time_rows[part_rows:])
    combined = 0.5 * (even_re + twist_re * odd_re + twist_im * odd_im)
    conv_part = combined[:channels_dev]
    corr_part = combined[channels_dev : 2 * channels_dev]
    filter_local = combined[2 * channels_dev :]
    conv_out = conv_part + skip_gain[:, None] * gated_prod
    gated_grad = corr_part + skip_gain[:, None] * gate_grad
    members_total = channels_dev * lax.axis_size("chan") // filters
    filter_grad = lax.psum(filter_local, "chan") * (1.0 / math.sqrt(members_total * seq_total))
    grads_in = jnp.stack([out_float * conv_out, gated_grad * values, gated_grad * gate_in])
    following = shifted(grads_in[:, :, :reach_back], "seq", -1)
    extended_grad = jnp.concatenate([grads_in, following], axis=2)
    result = jnp.zeros(grads_in.shape, jnp.float32)
    for offset in range(tap_count):
        result = (
            result
            + short_filters[:, offset, :, None] * extended_grad[:, :, offset : offset + length]
        )
    return (result.astype(jnp.bfloat16), filter_grad)


BF16 = jnp.bfloat16
F32 = jnp.float32
LANES = 128
OPERANDS = 15


def split16(value):
    high = value.astype(BF16)
    return high, (value - high.astype(F32)).astype(BF16)


def host_split(table):
    high = table.astype(np.float32).astype(ml_dtypes.bfloat16)
    low = (table - high.astype(np.float64)).astype(np.float32).astype(ml_dtypes.bfloat16)
    return high, low


def one_hot_rows(sources):
    table = np.zeros((len(sources), len(sources)), np.float32)
    table[np.arange(len(sources)), sources] = 1.0
    return table.astype(ml_dtypes.bfloat16)


def tables(channels, filters, devices, tokens):
    members = channels // filters
    own_filters = filters // devices
    rows = np.arange(channels)
    block = channels // devices
    owner, side, within = rows // block, rows // (block // 2) % 2, rows % (block // 2)
    gather = np.zeros((2, channels, 2 * channels), np.float32)
    scatter = np.zeros((2, channels, 2 * channels), np.float32)
    for chunk in range(2):
        own = chunk * own_filters // 2 + within // members
        channel = filters * (within % members) + own_filters * owner + own
        gather[chunk, rows, side * channels + channel] = 1.0
        scatter[side, channel, chunk * channels + rows] = 1.0
    gather, scatter = gather.astype(ml_dtypes.bfloat16), scatter.astype(ml_dtypes.bfloat16)
    rows = np.arange(4 * filters)
    owner, kind, own = rows // (4 * own_filters), rows // own_filters % 4, rows % own_filters
    filter_order = one_hot_rows(kind * filters + owner * own_filters + own)
    fft_size = 2 * tokens
    outer = fft_size // LANES
    used = outer // 2
    angle = 2.0 * math.pi * (np.outer(np.arange(outer), np.arange(used)) % outer) / outer
    cosine, sine = np.cos(angle), np.sin(angle)
    first = np.block([[cosine, sine], [-sine, cosine]])
    high, low = host_split(first)
    first_cat = np.concatenate([high, low, high], axis=1)
    high, low = high[:, :used], low[:, :used]
    first_real = np.concatenate([high, low, high], axis=1)
    last = np.block([[cosine.T, -sine.T], [sine.T, cosine.T]]) / fft_size
    high, low = host_split(last)
    last_cat = np.concatenate([high, low, high], axis=1)
    angle = 2.0 * math.pi * (np.outer(np.arange(LANES), np.arange(LANES)) % LANES) / LANES
    cosine, sine = np.cos(angle), np.sin(angle)
    inner = np.stack(host_split(np.block([[cosine, -sine], [sine, cosine]])))
    inner_back = np.stack(host_split(np.block([[cosine, sine], [-sine, cosine]])))
    angle = -2.0 * math.pi * np.outer(np.arange(outer), np.arange(LANES)) / fft_size
    twiddles = np.stack([np.cos(angle), np.sin(angle)]).astype(np.float32)
    return (
        gather,
        scatter,
        filter_order,
        np.ascontiguousarray(filter_order.T),
        first_cat,
        first_real,
        last_cat,
        inner,
        inner_back,
        twiddles,
    )


def dot32(left, right):
    return jnp.dot(left, right, preferred_element_type=F32)


def inner_product(value, table_ref):
    high, low = split16(value)
    return dot32(high, table_ref[0]) + dot32(low, table_ref[0]) + dot32(high, table_ref[1])


def outer_product(table, value):
    high, low = split16(value)
    return dot32(table, jnp.concatenate([high, high, low], axis=0))


def halves_of(value):
    return value[:, :LANES], value[:, LANES:]


def product(first, second, conjugate):
    a, b = halves_of(first)
    c, d = halves_of(second)
    if conjugate:
        return jnp.concatenate([a * c + b * d, b * c - a * d], axis=1)
    return jnp.concatenate([a * c - b * d, a * d + b * c], axis=1)


def delayed(value, by):
    if by == 0:
        return value
    zeros = jnp.zeros((value.shape[0], LANES), F32)
    return pltpu.roll(jnp.concatenate([zeros, value], axis=1), by, 1)[:, LANES:]


def advanced(value, by):
    if by == 0:
        return value
    length = value.shape[1]
    zeros = jnp.zeros((value.shape[0], LANES), F32)
    return pltpu.roll(jnp.concatenate([value, zeros], axis=1), length + LANES - by, 1)[:, :length]


def kernel(filter_scale, *refs):
    operands, refs = refs[:OPERANDS], refs[OPERANDS:]
    stream_grad, filter_grad = refs[:2]
    (
        streams,
        out_grad,
        long_filter,
        short_filters,
        skip_gain,
        gather,
        scatter,
        filter_order,
        filter_order_t,
        first_cat,
        first_real,
        last_cat,
        inner,
        inner_back,
        twiddles,
    ) = locals_ = refs[2 : 2 + OPERANDS]
    (
        sent_zero,
        sent_one,
        held_zero,
        held_one,
        answers_zero,
        answers_one,
        results_zero,
        results_one,
        signal_rows,
        filter_rows,
        own_part,
        other_part,
        send_sem,
        recv_sem,
        back_send_sem,
        back_recv_sem,
        part_sem,
        load_sem,
        gather_sem,
    ) = refs[2 + OPERANDS :]
    devices = sent_one.shape[0]
    rows = sent_one.shape[1]
    half = rows // 2
    channels, length = streams.shape[1:]
    filters = long_filter.shape[0]
    taps = short_filters.shape[1]
    own_filters = filters // devices
    chunk_filters = own_filters // 2
    members = rows // own_filters
    pairs = half // 2
    per_filter = members // 2
    used = devices * length // LANES
    outer = 2 * used
    pieces = length // LANES
    sent, held = (sent_zero, sent_one), (held_zero, held_one)
    answers, results = (answers_zero, answers_one), (results_zero, results_one)
    me = lax.axis_index("seq")
    other = 1 - lax.axis_index("chan")

    barrier = pltpu.get_barrier_semaphore()
    for step in range(1, devices):
        pl.semaphore_signal(
            barrier, inc=1, device_id={"seq": lax.rem(me + step, devices)}, device_id_type=MESH
        )
    pl.semaphore_signal(barrier, inc=1, device_id={"chan": other}, device_id_type=MESH)

    loads = [
        pltpu.make_async_copy(operands[index], locals_[index], load_sem.at[index])
        for index in range(OPERANDS)
    ]
    gather_place = 5
    gather_loads = [
        pltpu.make_async_copy(
            operands[gather_place].at[chunk], gather.at[chunk], gather_sem.at[chunk]
        )
        for chunk in range(2)
    ]
    first = (0, 1, 7, 2)
    later = [index for index in range(OPERANDS) if index not in first + (gather_place,)]
    gather_loads[0].start()
    for index in first:
        loads[index].start()
    gather_loads[1].start()
    gather_loads[0].wait()
    for index in first:
        loads[index].wait()

    blocks = (
        jnp.concatenate([streams[0], streams[2]], axis=0),
        jnp.concatenate([streams[1], out_grad[...]], axis=0),
    )

    def fill(chunk):
        for index in range(2):
            moved = dot32(gather[chunk], blocks[index]).astype(BF16)
            sent[chunk][:, :, index * length : (index + 1) * length] = moved.reshape(
                devices, rows, length
            )

    def exchange(source, target, send, recv, chunk):
        copies = []
        for step in range(1, devices):
            peer = lax.rem(me + step, devices)
            copy = pltpu.make_async_remote_copy(
                src_ref=source.at[peer],
                dst_ref=target.at[me],
                send_sem=send.at[chunk, peer],
                recv_sem=recv.at[chunk, me],
                device_id={"seq": peer},
                device_id_type=MESH,
            )
            copy.start()
            copies.append(copy)
        target[me] = source[me]
        return copies

    def finish(source, target, send, recv, chunk):
        for step in range(1, devices):
            peer = lax.rem(me + step, devices)
            pltpu.make_async_remote_copy(
                src_ref=source.at[peer],
                dst_ref=target.at[peer],
                send_sem=send.at[chunk, peer],
                recv_sem=recv.at[chunk, peer],
                device_id={"seq": peer},
                device_id_type=MESH,
            ).wait_recv()

    fill(0)
    high, low = split16(long_filter[...])
    stacked = []
    for piece in range(pieces):
        columns = slice(piece * LANES, (piece + 1) * LANES)
        stacked += [high[:, columns], low[:, columns]]
    moved = dot32(filter_order[...], jnp.concatenate(stacked, axis=0)).astype(BF16)
    sent_zero[:, :, 2 * length :] = moved.reshape(devices, rows, LANES)
    pl.semaphore_wait(barrier, devices)
    copies = exchange(sent_zero, held_zero, send_sem, recv_sem, 0)
    for index in later:
        loads[index].start()
    gather_loads[1].wait()
    fill(1)
    copies += exchange(sent_one, held_one, send_sem, recv_sem, 1)

    for index in later:
        loads[index].wait()
    own_rows = pl.ds(pl.multiple_of(me * rows, rows), rows)
    picked = jnp.concatenate(
        [gather[chunk, own_rows, :channels].astype(F32)[:half] for chunk in range(2)], axis=0
    )

    def own_columns(values):
        return lax.dot_general(
            picked,
            values,
            (((1,), (1,)), ((), ())),
            precision=lax.Precision.HIGHEST,
            preferred_element_type=F32,
        )

    all_weights = [own_columns(short_filters[index]) for index in range(3)]
    all_gain = jnp.sum(picked * skip_gain[...], axis=1, keepdims=True)
    twiddle_re, twiddle_im = twiddles[0], twiddles[1]

    def forward(outer_out):
        turned = []
        for index in range(outer_out.shape[1] // LANES):
            columns = slice(index * LANES, (index + 1) * LANES)
            real_part, imag_part = outer_out[:outer, columns], outer_out[outer:, columns]
            turned.append(
                jnp.concatenate(
                    [
                        real_part * twiddle_re - imag_part * twiddle_im,
                        real_part * twiddle_im + imag_part * twiddle_re,
                    ],
                    axis=1,
                )
            )
        return inner_product(jnp.concatenate(turned, axis=0), inner)

    def spectrum(spectra, index):
        return spectra[index * outer : (index + 1) * outer]

    def inverse(values, table):
        inner_out = inner_product(jnp.concatenate(values, axis=0), inner_back)
        columns = []
        for index in range(len(values)):
            real_part, imag_part = halves_of(inner_out[index * outer : (index + 1) * outer])
            columns.append(
                jnp.concatenate(
                    [
                        real_part * twiddle_re + imag_part * twiddle_im,
                        imag_part * twiddle_re - real_part * twiddle_im,
                    ],
                    axis=0,
                )
            )
        return outer_product(table, jnp.concatenate(columns, axis=1))

    def filter_spectra():
        for source in range(devices):
            filter_rows[source * rows : (source + 1) * rows, :] = held_zero[
                source, :, 2 * length :
            ].astype(F32)
        high, low = [
            jnp.concatenate(
                [
                    filter_rows[pl.ds(part * own_filters + own, used, stride=stride), :]
                    for own in range(own_filters)
                ],
                axis=1,
            ).astype(BF16)
            for part in range(2)
        ]
        return forward(dot32(first_real[...], jnp.concatenate([high, high, low], axis=0)))

    stride = 2 * own_filters

    def work(chunk, filter_specs):
        weights = [value[chunk * half : (chunk + 1) * half] for value in all_weights]
        gain = all_gain[chunk * half : (chunk + 1) * half]
        received = held[chunk]

        def whole(side, index):
            columns = slice(index * length, (index + 1) * length)
            return jnp.concatenate(
                [
                    received[source, :, columns].astype(F32)[side * half : (side + 1) * half]
                    for source in range(devices)
                ],
                axis=1,
            )

        filtered = []
        for index, place in enumerate(((0, 0), (0, 1), (1, 0))):
            value = whole(*place)
            total = weights[index][:, 0:1] * value
            for offset in range(1, taps):
                total = total + weights[index][:, offset : offset + 1] * delayed(value, offset)
            filtered.append(total)
        out_float = whole(1, 1)
        gated_prod = filtered[1] * filtered[2]
        gate_grad = out_float * filtered[0]
        for block in range(used):
            columns = slice(block * LANES, (block + 1) * LANES)
            span = slice(block * half, (block + 1) * half)
            signal_rows[chunk, 0, span, :] = gated_prod[:, columns]
            signal_rows[chunk, 1, span, :] = gate_grad[:, columns]

        def packed(which, part):
            return [
                signal_rows[chunk, which, pl.ds(2 * pair + part, used, stride=half), :]
                for pair in range(pairs)
            ]

        signals = jnp.concatenate(
            [jnp.concatenate(packed(0, part) + packed(1, part), axis=1) for part in range(2)],
            axis=0,
        )
        spectra = forward(outer_product(first_cat[...], signals))
        sums = []
        for own in range(chunk_filters):
            total = None
            for index in range(own * per_filter, (own + 1) * per_filter):
                term = product(spectrum(spectra, pairs + index), spectrum(spectra, index), True)
                total = term if total is None else total + term
            sums.append(total)
        own_part[chunk] = inverse(sums, last_cat[:used, :])
        part_copy = pltpu.make_async_remote_copy(
            src_ref=own_part.at[chunk],
            dst_ref=other_part.at[chunk],
            send_sem=part_sem.at[0, chunk],
            recv_sem=part_sem.at[1, chunk],
            device_id={"chan": other},
            device_id_type=MESH,
        )
        part_copy.start()

        products = []
        for index in range(2 * pairs):
            own = chunk * chunk_filters + index % pairs // per_filter
            products.append(
                product(spectrum(spectra, index), spectrum(filter_specs, own), index >= pairs)
            )
        times = inverse(products, last_cat[...])
        for index in range(2 * pairs):
            which, pair = index // pairs, index % pairs
            columns = slice(index * LANES, (index + 1) * LANES)
            for part in range(2):
                signal_rows[chunk, which, pl.ds(2 * pair + part, used, stride=half), :] = times[
                    part * used : (part + 1) * used, columns
                ]

        def joined(which):
            return jnp.concatenate(
                [
                    signal_rows[chunk, which, block * half : (block + 1) * half, :]
                    for block in range(used)
                ],
                axis=1,
            )

        conv_out = joined(0) + gain * gated_prod
        gated_grad = joined(1) + gain * gate_grad
        grads = (out_float * conv_out, gated_grad * filtered[2], gated_grad * filtered[1])
        totals = []
        for index in range(3):
            value = grads[index]
            total = weights[index][:, 0:1] * value
            for offset in range(1, taps):
                total = total + weights[index][:, offset : offset + 1] * advanced(value, offset)
            totals.append(total)
        both = jnp.concatenate(totals[:2], axis=0).astype(BF16)
        for target in range(devices):
            start = target * length
            answers[chunk][target, :, :length] = both[:, start : start + length]
            answers[chunk][target, :, length : length + LANES] = jnp.concatenate(
                [
                    totals[2][:, start : start + LANES],
                    totals[2][:, start + LANES : start + 2 * LANES],
                ],
                axis=0,
            ).astype(BF16)
        return part_copy

    finish(sent_zero, held_zero, send_sem, recv_sem, 0)
    filter_specs = filter_spectra()
    part_copies = [work(0, filter_specs)]
    back_copies = exchange(answers_zero, results_zero, back_send_sem, back_recv_sem, 0)
    finish(sent_one, held_one, send_sem, recv_sem, 1)
    part_copies.append(work(1, filter_specs))

    for copy in part_copies:
        copy.wait()
    for chunk in range(2):
        high, low = split16((own_part[chunk] + other_part[chunk]) * filter_scale)
        for index in range(chunk_filters):
            columns = slice(index * LANES, (index + 1) * LANES)
            own = chunk * chunk_filters + index
            filter_rows[pl.ds(own, used, stride=stride), :] = high[:, columns].astype(F32)
            filter_rows[pl.ds(own_filters + own, used, stride=stride), :] = low[
                :, columns
            ].astype(F32)
    for target in range(devices):
        answers_one[target, :, length + LANES :] = filter_rows[
            target * rows : (target + 1) * rows, :
        ].astype(BF16)
    back_copies += exchange(answers_one, results_one, back_send_sem, back_recv_sem, 1)
    for copy in copies:
        copy.wait_send()
    for chunk in range(2):
        finish(answers[chunk], results[chunk], back_send_sem, back_recv_sem, chunk)

    def returned(columns):
        return jnp.concatenate(
            [results[chunk][:, :, columns].reshape(devices * rows, -1) for chunk in range(2)],
            axis=0,
        )

    for side in range(2):
        stream_grad[side] = dot32(scatter[side], returned(slice(0, length))).astype(BF16)
        stream_grad[2, :, side * LANES : (side + 1) * LANES] = dot32(
            scatter[side], returned(slice(length, length + LANES))
        ).astype(BF16)
    block = results_one[:, :, length + LANES :].reshape(devices * rows, LANES)
    moved = dot32(filter_order_t[...], block)
    for piece in range(pieces):
        start = 2 * piece * filters
        filter_grad[:, piece * LANES : (piece + 1) * LANES] = (
            moved[start : start + filters] + moved[start + filters : start + 2 * filters]
        )
    for copy in back_copies:
        copy.wait_send()


def fast_local(streams, short_filters, long_filter, skip_gain, out_grad):
    devices = lax.axis_size("seq")
    channels, length = streams.shape[1:]
    filters = long_filter.shape[0]
    tokens = devices * length
    rows = channels // devices
    own_filters = filters // devices
    used = tokens // LANES
    members_total = channels * lax.axis_size("chan") // filters
    constants = [jnp.asarray(table) for table in tables(channels, filters, devices, tokens)]
    arguments = [
        streams,
        out_grad,
        long_filter,
        short_filters,
        skip_gain.reshape(1, channels),
    ] + constants
    vmem = pl.BlockSpec(memory_space=pltpu.VMEM)
    return pl.pallas_call(
        functools.partial(kernel, 1.0 / math.sqrt(members_total * tokens)),
        out_shape=(
            jax.ShapeDtypeStruct(streams.shape, BF16),
            jax.ShapeDtypeStruct(long_filter.shape, F32),
        ),
        in_specs=[pl.BlockSpec(memory_space=pltpu.HBM)] * len(arguments),
        out_specs=(vmem, vmem),
        scratch_shapes=[pltpu.VMEM(value.shape, value.dtype) for value in arguments]
        + [
            pltpu.VMEM((devices, rows, 2 * length + LANES), BF16),
            pltpu.VMEM((devices, rows, 2 * length), BF16),
            pltpu.VMEM((devices, rows, 2 * length + LANES), BF16),
            pltpu.VMEM((devices, rows, 2 * length), BF16),
            pltpu.VMEM((devices, rows, length + LANES), BF16),
            pltpu.VMEM((devices, rows, length + 2 * LANES), BF16),
            pltpu.VMEM((devices, rows, length + LANES), BF16),
            pltpu.VMEM((devices, rows, length + 2 * LANES), BF16),
            pltpu.VMEM((2, 2, used * rows // 2, LANES), F32),
            pltpu.VMEM((devices * rows, LANES), F32),
            pltpu.VMEM((2, used, own_filters // 2 * LANES), F32),
            pltpu.VMEM((2, used, own_filters // 2 * LANES), F32),
            pltpu.SemaphoreType.DMA((2, devices)),
            pltpu.SemaphoreType.DMA((2, devices)),
            pltpu.SemaphoreType.DMA((2, devices)),
            pltpu.SemaphoreType.DMA((2, devices)),
            pltpu.SemaphoreType.DMA((2, 2)),
            pltpu.SemaphoreType.DMA((OPERANDS,)),
            pltpu.SemaphoreType.DMA((2,)),
        ],
        compiler_params=pltpu.CompilerParams(
            collective_id=0, has_side_effects=True, vmem_limit_bytes=62 * 2**20
        ),
    )(*arguments)


def fits_fast(mesh, channels, tokens, filters):
    devices, groups = mesh.shape["seq"], mesh.shape["chan"]
    channels, length = channels // groups, tokens // devices
    if groups != 2 or filters % devices or channels % (2 * filters) or channels % (16 * devices):
        return False
    return length == 2 * LANES and channels // devices == 4 * (filters // devices) == 16


def solution(mesh):
    in_specs = (
        P(None, "chan", "seq"),
        P(None, None, "chan"),
        P(None, "seq"),
        P("chan"),
        P("chan", "seq"),
    )
    out_specs = (P(None, "chan", "seq"), P(None, "seq"))

    def whole_program(streams, short_filters, long_filter, skip_gain, out_grad):
        fast = fits_fast(mesh, streams.shape[1], streams.shape[2], long_filter.shape[0])
        return jax.shard_map(
            fast_local if fast else local,
            mesh=mesh,
            in_specs=in_specs,
            out_specs=out_specs,
            check_vma=False,
        )(streams, short_filters, long_filter, skip_gain, out_grad)

    return whole_program
```

```python
import functools
import math

import jax
import jax.numpy as jnp
import ml_dtypes
import numpy as np
from jax import lax
from jax.experimental import pallas as pl
from jax.experimental.pallas import tpu as pltpu
from jax.sharding import PartitionSpec as P

MESH = pl.DeviceIdType.MESH


def partner_2(value, axis, apart):
    mask = 2**apart
    pairs = [(source, source ^ mask) for source in range(lax.axis_size(axis))]
    return lax.ppermute(value, axis, pairs)


def shifted(shard, axis, by):
    length = lax.axis_size(axis)
    pairs = [(i, i + by) for i in range(length) if 0 <= i + by < length]
    return lax.ppermute(shard, axis, pairs)


def rotate(real_part, imag_part, cosine, sine_part):
    return (real_part * cosine - imag_part * sine_part, real_part * sine_part + imag_part * cosine)


def split_halves(signal):
    middle = signal.shape[-1] // 2
    return (signal[..., :middle], signal[..., middle:])


def join_halves(real_part, imag_part):
    return jnp.concatenate([real_part, imag_part], axis=-1)


def complex_product(first_op, second_op, conjugate):
    first_re, first_im = split_halves(first_op)
    second_re, second_im = split_halves(second_op)
    if conjugate:
        second_im = -second_im
    return join_halves(
        first_re * second_re - first_im * second_im, first_re * second_im + first_im * second_re
    )


def dft_table(length, direction, scaling):
    indices = jnp.arange(length, dtype=jnp.int32)
    phases = (indices[:, None] * indices[None, :] % length).astype(jnp.float32) * (
        direction * 2.0 * math.pi / length
    )
    cosine = jnp.cos(phases) * scaling
    sine_part = jnp.sin(phases) * scaling
    upper_rows = jnp.concatenate([cosine, sine_part], axis=1)
    lower_rows = jnp.concatenate([-sine_part, cosine], axis=1)
    return jnp.concatenate([upper_rows, lower_rows], axis=0)


def section_count():
    return lax.axis_size("seq").bit_length() - 1


def bit_reverse(position, sections):
    result = jnp.zeros((), jnp.int32)
    for bit_level in range(sections):
        result = result + position // (1 << bit_level) % 2 * (1 << sections - 1 - bit_level)
    return result


def held_index():
    return bit_reverse(lax.axis_index("seq"), section_count())


def inner_twiddle(signal, held, direction):
    length = signal.shape[-1] // 2
    seq_total = length * lax.axis_size("seq")
    indices = jnp.arange(length, dtype=jnp.int32)
    phases = (indices * held % seq_total).astype(jnp.float32) * (
        direction * 2.0 * math.pi / seq_total
    )
    real_part, imag_part = split_halves(signal)
    turned_re, turned_im = rotate(real_part, imag_part, jnp.cos(phases), jnp.sin(phases))
    return join_halves(turned_re, turned_im)


def forward_sections(signal):
    position = lax.axis_index("seq")
    sections = section_count()
    for bit_level in reversed(range(sections)):
        half_span = 1 << bit_level
        partner = partner_2(signal, "seq", bit_level)
        upper_side = position // half_span % 2 == 1
        phases = (position % half_span).astype(jnp.float32) * (-math.pi / half_span)
        diff_re, diff_im = split_halves(partner - signal)
        turned_re, turned_im = rotate(diff_re, diff_im, jnp.cos(phases), jnp.sin(phases))
        signal = jnp.where(upper_side, join_halves(turned_re, turned_im), signal + partner)
    return signal


def inverse_sections(signal):
    position = lax.axis_index("seq")
    sections = section_count()
    for bit_level in range(sections):
        half_span = 1 << bit_level
        partner = partner_2(signal, "seq", bit_level)
        upper_side = position // half_span % 2 == 1
        phases = (position % half_span).astype(jnp.float32) * (math.pi / half_span)
        source = jnp.where(upper_side, signal, partner)
        base_term = jnp.where(upper_side, partner, signal)
        source_re, source_im = split_halves(source)
        turned_re, turned_im = rotate(source_re, source_im, jnp.cos(phases), jnp.sin(phases))
        turned = join_halves(turned_re, turned_im)
        signal = 0.5 * jnp.where(upper_side, base_term - turned, base_term + turned)
    return signal


def forward_dft(signal, dft_matrix):
    signal = forward_sections(signal)
    signal = inner_twiddle(signal, held_index(), -1.0)
    return jnp.dot(
        signal, dft_matrix, precision=lax.Precision.HIGHEST, preferred_element_type=jnp.float32
    )


def inverse_dft(spectra, dft_matrix):
    signal = jnp.dot(
        spectra, dft_matrix, precision=lax.Precision.HIGHEST, preferred_element_type=jnp.float32
    )
    signal = inner_twiddle(signal, held_index(), 1.0)
    return inverse_sections(signal)


def local(streams, short_filters, long_filter, skip_gain, out_grad):
    tap_count = short_filters.shape[1]
    reach_back = tap_count - 1
    channels_dev = streams.shape[1]
    length = streams.shape[2]
    filters = long_filter.shape[0]
    members = channels_dev // filters
    devices = lax.axis_size("seq")
    position = lax.axis_index("seq")
    seq_total = length * devices
    preceding = shifted(streams[:, :, length - reach_back :], "seq", 1)
    extended = jnp.concatenate([preceding, streams], axis=2).astype(jnp.float32)
    filtered = jnp.zeros(streams.shape, jnp.float32)
    for offset in range(tap_count):
        filtered = (
            filtered
            + short_filters[:, offset, :, None]
            * extended[:, :, reach_back - offset : reach_back - offset + length]
        )
    gate_out = filtered[0]
    gate_in = filtered[1]
    values = filtered[2]
    gated_prod = gate_in * values
    out_float = out_grad.astype(jnp.float32)
    gate_grad = out_float * gate_out
    signals = jnp.concatenate([gated_prod, gate_grad, long_filter], axis=0)
    twist_phase = (position * length + jnp.arange(length, dtype=jnp.int32)).astype(jnp.float32) * (
        -math.pi / seq_total
    )
    twist_re = jnp.cos(twist_phase)
    twist_im = jnp.sin(twist_phase)
    even_part = join_halves(signals, jnp.zeros_like(signals))
    odd_part = join_halves(signals * twist_re, signals * twist_im)
    spectra = forward_dft(
        jnp.concatenate([even_part, odd_part], axis=0), dft_table(length, -1.0, 1.0)
    )
    row_count = signals.shape[0]
    halves = (spectra[:row_count], spectra[row_count:])
    filter_specs = (halves[0][2 * channels_dev :], halves[1][2 * channels_dev :])
    products = []
    for half_index in range(2):
        part_spec = halves[half_index]
        gated_spec = part_spec[:channels_dev]
        grad_spec = part_spec[channels_dev : 2 * channels_dev]
        wide_filter = jnp.tile(filter_specs[half_index], (members, 1))
        products.append(complex_product(gated_spec, wide_filter, False))
        products.append(complex_product(grad_spec, wide_filter, True))
        products.append(
            complex_product(grad_spec, gated_spec, True)
            .reshape(members, filters, 2 * length)
            .sum(axis=0)
        )
    time_rows = inverse_dft(jnp.concatenate(products, axis=0), dft_table(length, 1.0, 1.0 / length))
    part_rows = 2 * channels_dev + filters
    even_re, even_im = split_halves(time_rows[:part_rows])
    odd_re, odd_im = split_halves(time_rows[part_rows:])
    combined = 0.5 * (even_re + twist_re * odd_re + twist_im * odd_im)
    conv_part = combined[:channels_dev]
    corr_part = combined[channels_dev : 2 * channels_dev]
    filter_local = combined[2 * channels_dev :]
    conv_out = conv_part + skip_gain[:, None] * gated_prod
    gated_grad = corr_part + skip_gain[:, None] * gate_grad
    members_total = channels_dev * lax.axis_size("chan") // filters
    filter_grad = lax.psum(filter_local, "chan") * (1.0 / math.sqrt(members_total * seq_total))
    grads_in = jnp.stack([out_float * conv_out, gated_grad * values, gated_grad * gate_in])
    following = shifted(grads_in[:, :, :reach_back], "seq", -1)
    extended_grad = jnp.concatenate([grads_in, following], axis=2)
    result = jnp.zeros(grads_in.shape, jnp.float32)
    for offset in range(tap_count):
        result = (
            result
            + short_filters[:, offset, :, None] * extended_grad[:, :, offset : offset + length]
        )
    return (result.astype(jnp.bfloat16), filter_grad)


BF16 = jnp.bfloat16
F32 = jnp.float32
LANES = 128
OPERANDS = 15


def split16(value):
    high = value.astype(BF16)
    return high, (value - high.astype(F32)).astype(BF16)


def host_split(table):
    high = table.astype(np.float32).astype(ml_dtypes.bfloat16)
    low = (table - high.astype(np.float64)).astype(np.float32).astype(ml_dtypes.bfloat16)
    return high, low


def one_hot_rows(sources):
    table = np.zeros((len(sources), len(sources)), np.float32)
    table[np.arange(len(sources)), sources] = 1.0
    return table.astype(ml_dtypes.bfloat16)


def tables(channels, filters, devices, tokens):
    members = channels // filters
    own_filters = filters // devices
    rows = np.arange(channels)
    block = channels // devices
    owner, side, within = rows // block, rows // (block // 2) % 2, rows % (block // 2)
    gather = np.zeros((2, channels, 2 * channels), np.float32)
    scatter = np.zeros((2, channels, 2 * channels), np.float32)
    for chunk in range(2):
        own = chunk * own_filters // 2 + within // members
        channel = filters * (within % members) + own_filters * owner + own
        gather[chunk, rows, side * channels + channel] = 1.0
        scatter[side, channel, chunk * channels + rows] = 1.0
    gather, scatter = gather.astype(ml_dtypes.bfloat16), scatter.astype(ml_dtypes.bfloat16)
    rows = np.arange(4 * filters)
    owner, kind, own = rows // (4 * own_filters), rows // own_filters % 4, rows % own_filters
    filter_order = one_hot_rows(kind * filters + owner * own_filters + own)
    fft_size = 2 * tokens
    outer = fft_size // LANES
    used = outer // 2
    angle = 2.0 * math.pi * (np.outer(np.arange(outer), np.arange(used)) % outer) / outer
    cosine, sine = np.cos(angle), np.sin(angle)
    first = np.block([[cosine, sine], [-sine, cosine]])
    high, low = host_split(first)
    first_cat = np.concatenate([high, low, high], axis=1)
    high, low = high[:, :used], low[:, :used]
    first_real = np.concatenate([high, low, high], axis=1)
    last = np.block([[cosine.T, -sine.T], [sine.T, cosine.T]]) / fft_size
    high, low = host_split(last)
    last_cat = np.concatenate([high, low, high], axis=1)
    angle = 2.0 * math.pi * (np.outer(np.arange(LANES), np.arange(LANES)) % LANES) / LANES
    cosine, sine = np.cos(angle), np.sin(angle)
    inner = np.stack(host_split(np.block([[cosine, -sine], [sine, cosine]])))
    inner_back = np.stack(host_split(np.block([[cosine, sine], [-sine, cosine]])))
    angle = -2.0 * math.pi * np.outer(np.arange(outer), np.arange(LANES)) / fft_size
    twiddles = np.stack([np.cos(angle), np.sin(angle)]).astype(np.float32)
    return (
        gather,
        scatter,
        filter_order,
        np.ascontiguousarray(filter_order.T),
        first_cat,
        first_real,
        last_cat,
        inner,
        inner_back,
        twiddles,
    )


def dot32(left, right):
    return jnp.dot(left, right, preferred_element_type=F32)


def inner_product(value, table_ref):
    high, low = split16(value)
    return dot32(high, table_ref[0]) + dot32(low, table_ref[0]) + dot32(high, table_ref[1])


def outer_product(table, value):
    high, low = split16(value)
    return dot32(table, jnp.concatenate([high, high, low], axis=0))


def halves_of(value):
    return value[:, :LANES], value[:, LANES:]


def product(first, second, conjugate):
    a, b = halves_of(first)
    c, d = halves_of(second)
    if conjugate:
        return jnp.concatenate([a * c + b * d, b * c - a * d], axis=1)
    return jnp.concatenate([a * c - b * d, a * d + b * c], axis=1)


def delayed(value, by):
    if by == 0:
        return value
    zeros = jnp.zeros((value.shape[0], LANES), F32)
    return pltpu.roll(jnp.concatenate([zeros, value], axis=1), by, 1)[:, LANES:]


def advanced(value, by):
    if by == 0:
        return value
    length = value.shape[1]
    zeros = jnp.zeros((value.shape[0], LANES), F32)
    return pltpu.roll(jnp.concatenate([value, zeros], axis=1), length + LANES - by, 1)[:, :length]


def kernel(filter_scale, *refs):
    operands, refs = refs[:OPERANDS], refs[OPERANDS:]
    stream_grad, filter_grad = refs[:2]
    (
        streams,
        out_grad,
        long_filter,
        short_filters,
        skip_gain,
        gather,
        scatter,
        filter_order,
        filter_order_t,
        first_cat,
        first_real,
        last_cat,
        inner,
        inner_back,
        twiddles,
    ) = locals_ = refs[2 : 2 + OPERANDS]
    (
        sent_zero,
        sent_one,
        held_zero,
        held_one,
        answers_zero,
        answers_one,
        results_zero,
        results_one,
        signal_rows,
        filter_rows,
        own_part,
        other_part,
        send_sem,
        recv_sem,
        back_send_sem,
        back_recv_sem,
        part_sem,
        load_sem,
        gather_sem,
    ) = refs[2 + OPERANDS :]
    devices = sent_one.shape[0]
    rows = sent_one.shape[1]
    half = rows // 2
    channels, length = streams.shape[1:]
    filters = long_filter.shape[0]
    taps = short_filters.shape[1]
    own_filters = filters // devices
    chunk_filters = own_filters // 2
    members = rows // own_filters
    pairs = half // 2
    per_filter = members // 2
    used = devices * length // LANES
    outer = 2 * used
    pieces = length // LANES
    sent, held = (sent_zero, sent_one), (held_zero, held_one)
    answers, results = (answers_zero, answers_one), (results_zero, results_one)
    me = lax.axis_index("seq")
    other = 1 - lax.axis_index("chan")

    barrier = pltpu.get_barrier_semaphore()
    for step in range(1, devices):
        pl.semaphore_signal(
            barrier, inc=1, device_id={"seq": lax.rem(me + step, devices)}, device_id_type=MESH
        )
    pl.semaphore_signal(barrier, inc=1, device_id={"chan": other}, device_id_type=MESH)

    loads = [
        pltpu.make_async_copy(operands[index], locals_[index], load_sem.at[index])
        for index in range(OPERANDS)
    ]
    gather_place = 5
    gather_loads = [
        pltpu.make_async_copy(
            operands[gather_place].at[chunk], gather.at[chunk], gather_sem.at[chunk]
        )
        for chunk in range(2)
    ]
    first = (0, 1, 7, 2)
    later = [index for index in range(OPERANDS) if index not in first + (gather_place,)]
    gather_loads[0].start()
    for index in first:
        loads[index].start()
    gather_loads[1].start()
    gather_loads[0].wait()
    for index in first:
        loads[index].wait()

    blocks = (
        jnp.concatenate([streams[0], streams[2]], axis=0),
        jnp.concatenate([streams[1], out_grad[...]], axis=0),
    )

    def fill(chunk):
        for index in range(2):
            moved = dot32(gather[chunk], blocks[index]).astype(BF16)
            sent[chunk][:, :, index * length : (index + 1) * length] = moved.reshape(
                devices, rows, length
            )

    def exchange(source, target, send, recv, chunk):
        copies = []
        for step in range(1, devices):
            peer = lax.rem(me + step + (1 - other) * (devices - 2 * step), devices)
            copy = pltpu.make_async_remote_copy(
                src_ref=source.at[peer],
                dst_ref=target.at[me],
                send_sem=send.at[chunk, peer],
                recv_sem=recv.at[chunk, me],
                device_id={"seq": peer},
                device_id_type=MESH,
            )
            copy.start()
            copies.append(copy)
        target[me] = source[me]
        return copies

    def finish(source, target, send, recv, chunk):
        for step in range(1, devices):
            peer = lax.rem(me + step + (1 - other) * (devices - 2 * step), devices)
            pltpu.make_async_remote_copy(
                src_ref=source.at[peer],
                dst_ref=target.at[peer],
                send_sem=send.at[chunk, peer],
                recv_sem=recv.at[chunk, peer],
                device_id={"seq": peer},
                device_id_type=MESH,
            ).wait_recv()

    fill(0)
    high, low = split16(long_filter[...])
    stacked = []
    for piece in range(pieces):
        columns = slice(piece * LANES, (piece + 1) * LANES)
        stacked += [high[:, columns], low[:, columns]]
    moved = dot32(filter_order[...], jnp.concatenate(stacked, axis=0)).astype(BF16)
    sent_zero[:, :, 2 * length :] = moved.reshape(devices, rows, LANES)
    pl.semaphore_wait(barrier, devices)
    copies = exchange(sent_zero, held_zero, send_sem, recv_sem, 0)
    for index in later:
        loads[index].start()
    gather_loads[1].wait()
    fill(1)
    copies += exchange(sent_one, held_one, send_sem, recv_sem, 1)

    for index in later:
        loads[index].wait()
    own_rows = pl.ds(pl.multiple_of(me * rows, rows), rows)
    picked = jnp.concatenate(
        [gather[chunk, own_rows, :channels].astype(F32)[:half] for chunk in range(2)], axis=0
    )

    def own_columns(values):
        return lax.dot_general(
            picked,
            values,
            (((1,), (1,)), ((), ())),
            precision=lax.Precision.HIGHEST,
            preferred_element_type=F32,
        )

    all_weights = [own_columns(short_filters[index]) for index in range(3)]
    all_gain = jnp.sum(picked * skip_gain[...], axis=1, keepdims=True)
    twiddle_re, twiddle_im = twiddles[0], twiddles[1]

    def forward(outer_out):
        turned = []
        for index in range(outer_out.shape[1] // LANES):
            columns = slice(index * LANES, (index + 1) * LANES)
            real_part, imag_part = outer_out[:outer, columns], outer_out[outer:, columns]
            turned.append(
                jnp.concatenate(
                    [
                        real_part * twiddle_re - imag_part * twiddle_im,
                        real_part * twiddle_im + imag_part * twiddle_re,
                    ],
                    axis=1,
                )
            )
        return inner_product(jnp.concatenate(turned, axis=0), inner)

    def spectrum(spectra, index):
        return spectra[index * outer : (index + 1) * outer]

    def inverse(values, table):
        inner_out = inner_product(jnp.concatenate(values, axis=0), inner_back)
        columns = []
        for index in range(len(values)):
            real_part, imag_part = halves_of(inner_out[index * outer : (index + 1) * outer])
            columns.append(
                jnp.concatenate(
                    [
                        real_part * twiddle_re + imag_part * twiddle_im,
                        imag_part * twiddle_re - real_part * twiddle_im,
                    ],
                    axis=0,
                )
            )
        return outer_product(table, jnp.concatenate(columns, axis=1))

    def filter_spectra():
        for source in range(devices):
            filter_rows[source * rows : (source + 1) * rows, :] = held_zero[
                source, :, 2 * length :
            ].astype(F32)
        high, low = [
            jnp.concatenate(
                [
                    filter_rows[pl.ds(part * own_filters + own, used, stride=stride), :]
                    for own in range(own_filters)
                ],
                axis=1,
            ).astype(BF16)
            for part in range(2)
        ]
        return forward(dot32(first_real[...], jnp.concatenate([high, high, low], axis=0)))

    stride = 2 * own_filters

    def work(chunk, filter_specs):
        weights = [value[chunk * half : (chunk + 1) * half] for value in all_weights]
        gain = all_gain[chunk * half : (chunk + 1) * half]
        received = held[chunk]

        def whole(side, index):
            columns = slice(index * length, (index + 1) * length)
            return jnp.concatenate(
                [
                    received[source, :, columns].astype(F32)[side * half : (side + 1) * half]
                    for source in range(devices)
                ],
                axis=1,
            )

        filtered = []
        for index, place in enumerate(((0, 0), (0, 1), (1, 0))):
            value = whole(*place)
            total = weights[index][:, 0:1] * value
            for offset in range(1, taps):
                total = total + weights[index][:, offset : offset + 1] * delayed(value, offset)
            filtered.append(total)
        out_float = whole(1, 1)
        gated_prod = filtered[1] * filtered[2]
        gate_grad = out_float * filtered[0]
        for block in range(used):
            columns = slice(block * LANES, (block + 1) * LANES)
            span = slice(block * half, (block + 1) * half)
            signal_rows[chunk, 0, span, :] = gated_prod[:, columns]
            signal_rows[chunk, 1, span, :] = gate_grad[:, columns]

        def packed(which, part):
            return [
                signal_rows[chunk, which, pl.ds(2 * pair + part, used, stride=half), :]
                for pair in range(pairs)
            ]

        signals = jnp.concatenate(
            [jnp.concatenate(packed(0, part) + packed(1, part), axis=1) for part in range(2)],
            axis=0,
        )
        spectra = forward(outer_product(first_cat[...], signals))
        sums = []
        for own in range(chunk_filters):
            total = None
            for index in range(own * per_filter, (own + 1) * per_filter):
                term = product(spectrum(spectra, pairs + index), spectrum(spectra, index), True)
                total = term if total is None else total + term
            sums.append(total)
        own_part[chunk] = inverse(sums, last_cat[:used, :])
        part_copy = pltpu.make_async_remote_copy(
            src_ref=own_part.at[chunk],
            dst_ref=other_part.at[chunk],
            send_sem=part_sem.at[0, chunk],
            recv_sem=part_sem.at[1, chunk],
            device_id={"chan": other},
            device_id_type=MESH,
        )
        part_copy.start()

        products = []
        for index in range(2 * pairs):
            own = chunk * chunk_filters + index % pairs // per_filter
            products.append(
                product(spectrum(spectra, index), spectrum(filter_specs, own), index >= pairs)
            )
        times = inverse(products, last_cat[...])
        for index in range(2 * pairs):
            which, pair = index // pairs, index % pairs
            columns = slice(index * LANES, (index + 1) * LANES)
            for part in range(2):
                signal_rows[chunk, which, pl.ds(2 * pair + part, used, stride=half), :] = times[
                    part * used : (part + 1) * used, columns
                ]

        def joined(which):
            return jnp.concatenate(
                [
                    signal_rows[chunk, which, block * half : (block + 1) * half, :]
                    for block in range(used)
                ],
                axis=1,
            )

        conv_out = joined(0) + gain * gated_prod
        gated_grad = joined(1) + gain * gate_grad
        grads = (out_float * conv_out, gated_grad * filtered[2], gated_grad * filtered[1])
        totals = []
        for index in range(3):
            value = grads[index]
            total = weights[index][:, 0:1] * value
            for offset in range(1, taps):
                total = total + weights[index][:, offset : offset + 1] * advanced(value, offset)
            totals.append(total)
        both = jnp.concatenate(totals[:2], axis=0).astype(BF16)
        for target in range(devices):
            start = target * length
            answers[chunk][target, :, :length] = both[:, start : start + length]
            answers[chunk][target, :, length : length + LANES] = jnp.concatenate(
                [
                    totals[2][:, start : start + LANES],
                    totals[2][:, start + LANES : start + 2 * LANES],
                ],
                axis=0,
            ).astype(BF16)
        return part_copy

    finish(sent_zero, held_zero, send_sem, recv_sem, 0)
    filter_specs = filter_spectra()
    part_copies = [work(0, filter_specs)]
    back_copies = exchange(answers_zero, results_zero, back_send_sem, back_recv_sem, 0)
    finish(sent_one, held_one, send_sem, recv_sem, 1)
    part_copies.append(work(1, filter_specs))

    for copy in part_copies:
        copy.wait()
    for chunk in range(2):
        high, low = split16((own_part[chunk] + other_part[chunk]) * filter_scale)
        for index in range(chunk_filters):
            columns = slice(index * LANES, (index + 1) * LANES)
            own = chunk * chunk_filters + index
            filter_rows[pl.ds(own, used, stride=stride), :] = high[:, columns].astype(F32)
            filter_rows[pl.ds(own_filters + own, used, stride=stride), :] = low[
                :, columns
            ].astype(F32)
    for target in range(devices):
        answers_one[target, :, length + LANES :] = filter_rows[
            target * rows : (target + 1) * rows, :
        ].astype(BF16)
    back_copies += exchange(answers_one, results_one, back_send_sem, back_recv_sem, 1)
    for copy in copies:
        copy.wait_send()
    for chunk in range(2):
        finish(answers[chunk], results[chunk], back_send_sem, back_recv_sem, chunk)

    def returned(columns):
        return jnp.concatenate(
            [results[chunk][:, :, columns].reshape(devices * rows, -1) for chunk in range(2)],
            axis=0,
        )

    for side in range(2):
        stream_grad[side] = dot32(scatter[side], returned(slice(0, length))).astype(BF16)
        stream_grad[2, :, side * LANES : (side + 1) * LANES] = dot32(
            scatter[side], returned(slice(length, length + LANES))
        ).astype(BF16)
    block = results_one[:, :, length + LANES :].reshape(devices * rows, LANES)
    moved = dot32(filter_order_t[...], block)
    for piece in range(pieces):
        start = 2 * piece * filters
        filter_grad[:, piece * LANES : (piece + 1) * LANES] = (
            moved[start : start + filters] + moved[start + filters : start + 2 * filters]
        )
    for copy in back_copies:
        copy.wait_send()


def fast_local(streams, short_filters, long_filter, skip_gain, out_grad):
    devices = lax.axis_size("seq")
    channels, length = streams.shape[1:]
    filters = long_filter.shape[0]
    tokens = devices * length
    rows = channels // devices
    own_filters = filters // devices
    used = tokens // LANES
    members_total = channels * lax.axis_size("chan") // filters
    constants = [jnp.asarray(table) for table in tables(channels, filters, devices, tokens)]
    arguments = [
        streams,
        out_grad,
        long_filter,
        short_filters,
        skip_gain.reshape(1, channels),
    ] + constants
    vmem = pl.BlockSpec(memory_space=pltpu.VMEM)
    return pl.pallas_call(
        functools.partial(kernel, 1.0 / math.sqrt(members_total * tokens)),
        out_shape=(
            jax.ShapeDtypeStruct(streams.shape, BF16),
            jax.ShapeDtypeStruct(long_filter.shape, F32),
        ),
        in_specs=[pl.BlockSpec(memory_space=pltpu.HBM)] * len(arguments),
        out_specs=(vmem, vmem),
        scratch_shapes=[pltpu.VMEM(value.shape, value.dtype) for value in arguments]
        + [
            pltpu.VMEM((devices, rows, 2 * length + LANES), BF16),
            pltpu.VMEM((devices, rows, 2 * length), BF16),
            pltpu.VMEM((devices, rows, 2 * length + LANES), BF16),
            pltpu.VMEM((devices, rows, 2 * length), BF16),
            pltpu.VMEM((devices, rows, length + LANES), BF16),
            pltpu.VMEM((devices, rows, length + 2 * LANES), BF16),
            pltpu.VMEM((devices, rows, length + LANES), BF16),
            pltpu.VMEM((devices, rows, length + 2 * LANES), BF16),
            pltpu.VMEM((2, 2, used * rows // 2, LANES), F32),
            pltpu.VMEM((devices * rows, LANES), F32),
            pltpu.VMEM((2, used, own_filters // 2 * LANES), F32),
            pltpu.VMEM((2, used, own_filters // 2 * LANES), F32),
            pltpu.SemaphoreType.DMA((2, devices)),
            pltpu.SemaphoreType.DMA((2, devices)),
            pltpu.SemaphoreType.DMA((2, devices)),
            pltpu.SemaphoreType.DMA((2, devices)),
            pltpu.SemaphoreType.DMA((2, 2)),
            pltpu.SemaphoreType.DMA((OPERANDS,)),
            pltpu.SemaphoreType.DMA((2,)),
        ],
        compiler_params=pltpu.CompilerParams(
            collective_id=0, has_side_effects=True, vmem_limit_bytes=62 * 2**20
        ),
    )(*arguments)


def fits_fast(mesh, channels, tokens, filters):
    devices, groups = mesh.shape["seq"], mesh.shape["chan"]
    channels, length = channels // groups, tokens // devices
    if groups != 2 or filters % devices or channels % (2 * filters) or channels % (16 * devices):
        return False
    return length == 2 * LANES and channels // devices == 4 * (filters // devices) == 16


def solution(mesh):
    in_specs = (
        P(None, "chan", "seq"),
        P(None, None, "chan"),
        P(None, "seq"),
        P("chan"),
        P("chan", "seq"),
    )
    out_specs = (P(None, "chan", "seq"), P(None, "seq"))

    def whole_program(streams, short_filters, long_filter, skip_gain, out_grad):
        fast = fits_fast(mesh, streams.shape[1], streams.shape[2], long_filter.shape[0])
        return jax.shard_map(
            fast_local if fast else local,
            mesh=mesh,
            in_specs=in_specs,
            out_specs=out_specs,
            check_vma=False,
        )(streams, short_filters, long_filter, skip_gain, out_grad)

    return whole_program
```
